32 devices in a mesh: scene: 2 (over x), tok: 16 (over z, y, core).
Axes of the slice: x: 2, y: 2, z: 4, core: 2. Of those that a mesh axis runs over, the one named last changes fastest.
Arguments:
- tokens: bfloat16 [16384, 768], P(('scene', 'tok')), parts along dimension 0, may hold values from -6 to 6
- qkv_weight: bfloat16 [768, 2304], replicated, may hold values from -0.21875 to 0.21875
- w_gate: float32 [4, 192, 384], replicated, may hold values from -0.4375 to 0.4375
- w_up: float32 [4, 192, 384], replicated, may hold values from -0.4375 to 0.4375
- w_down: float32 [4, 384, 192], replicated, may hold values from -0.3125 to 0.3125
- view_kind: int32 [32], P('scene'), parts along dimension 0, may hold values from 0 to 1, as said below
Outputs:
- mixed: bfloat16 [16384, 768], P(('scene', 'tok')), parts along dimension 0
The draws below stay inside these ranges and needn't reach their ends.
There are 2 independent parts, one for each index of `scene`. The reference program is written for one: setup_inputs(seed, part) draws one part's arguments, and reference() takes and returns one part's arrays. A program takes and returns all parts, laid end to end along the dimension named above; an argument that names none is the same for every part. Nothing has to cross between parts.
Inputs may be any that keep to these rules, and one draw needn't show every extreme that they name: `view_kind`: exactly 12 of the 16 views are input views.
All inputs are finite; a program needn't handle non-finite values.
Results may differ from the reference program's by a relative error of at most 0.03.
Values may be sent and summed in bfloat16 or wider, within the bound.
No kernel may reach another device: no remote copies, remote signals or barrier semaphores. Data moves between devices by JAX's collectives and lax.ppermute only.
A program may use at most 64 MiB of HBM per device.

```python
import jax
import jax.numpy as jnp
from jax import lax

D = 768
DH = 192
HID = 384
HEADS = 4
VIEWS = 16
NS_STEPS = 5
TOKENS = 8192
VIEW_TOK = 512


def draw_view_kind(key, part):
    order = jax.random.permutation(jax.random.fold_in(key, 7), VIEWS)
    return (order < 12).astype(jnp.int32)


def shard_levels(key, extent, pieces, least, high):
    factor_of = 1.0
    for position, blocks in pieces:
        heights = jax.random.uniform(jax.random.fold_in(jax.random.fold_in(key, 6), position), (blocks,), jnp.float32, least / len(pieces), high / len(pieces))
        factor_of = factor_of * jnp.repeat(jnp.exp(heights), extent[position] // blocks).reshape((-1,) + (1,) * (len(extent) - 1 - position))
    return factor_of


def gaussian(key, dims, scale, most, pieces=(), held_as=jnp.bfloat16):
    entries = scale * jax.random.normal(key, dims, jnp.float32)
    if pieces:
        entries = entries * shard_levels(key, dims, pieces, -0.22, 0.18)
    return jnp.clip(entries, -most, most).astype(held_as)


def setup_inputs(seed: int = 0, part: int = 0) -> dict:
    arg_keys = jax.random.split(jax.random.key(seed), 7)
    part_keys = jax.random.split(jax.random.fold_in(arg_keys[6], part), 7)
    tokens = gaussian(part_keys[0], (TOKENS, D), 1.0, 6.0, ((0, 16),))
    qkv_weight = gaussian(arg_keys[1], (D, 3 * D), D ** -0.5, 0.21875)
    w_gate = gaussian(arg_keys[2], (HEADS, DH, HID), DH ** -0.5, 0.4375, (), jnp.float32)
    w_up = gaussian(arg_keys[3], (HEADS, DH, HID), DH ** -0.5, 0.4375, (), jnp.float32)
    w_down = gaussian(arg_keys[4], (HEADS, HID, DH), HID ** -0.5, 0.3125, (), jnp.float32)
    view_kind = draw_view_kind(jax.random.fold_in(jax.random.fold_in(arg_keys[6], part), 71), part)
    return dict(tokens=tokens, qkv_weight=qkv_weight, w_gate=w_gate, w_up=w_up, w_down=w_down, view_kind=view_kind)


coef_a = 3.4445
coef_b = -4.775
coef_c = 2.0315
step_size = 0.8

def swish_parts(gate):
    sig = jax.nn.sigmoid(gate)
    return (gate * sig, sig * (1.0 + gate * (1.0 - sig)))

def newton(start):
    iterate = start
    for step in range(NS_STEPS):
        x32 = iterate.astype(jnp.float32)
        gram = jnp.einsum('mik,mjk->mij', x32, x32).astype(jnp.bfloat16)
        g32 = gram.astype(jnp.float32)
        square = jnp.einsum('mij,mjk->mik', g32, g32)
        mixer = (coef_b * g32 + coef_c * square).astype(jnp.bfloat16)
        iterate = (coef_a * x32 + jnp.einsum('mij,mjk->mik', mixer.astype(jnp.float32), x32)).astype(jnp.bfloat16)
    return iterate

def reference(tokens, qkv_weight, w_gate, w_up, w_down, view_kind):
    proj = jnp.dot(tokens, qkv_weight, preferred_element_type=jnp.float32).astype(jnp.bfloat16)
    query = proj[:, :D].reshape(TOKENS, HEADS, DH).astype(jnp.float32)
    keys = proj[:, D:2 * D].reshape(TOKENS, HEADS, DH).astype(jnp.float32)
    values = proj[:, 2 * D:].reshape(TOKENS, HEADS, DH)
    view_of = jnp.arange(TOKENS, dtype=jnp.int32) // VIEW_TOK
    flags = lax.optimization_barrier(jnp.sum(jnp.where(view_of[:, None] == jnp.arange(VIEWS, dtype=jnp.int32)[None, :], view_kind[None, :], 0), axis=1))
    masked = (values * flags.astype(jnp.bfloat16)[:, None, None]).astype(jnp.float32)
    gate_b = w_gate.astype(jnp.bfloat16).astype(jnp.float32)
    up_b = w_up.astype(jnp.bfloat16).astype(jnp.float32)
    down_b = w_down.astype(jnp.bfloat16).astype(jnp.float32)
    gate = jnp.einsum('thd,hdf->thf', keys, gate_b)
    upper = jnp.einsum('thd,hdf->thf', keys, up_b)
    act, slope = swish_parts(gate)
    hidden = (act * upper).astype(jnp.bfloat16).astype(jnp.float32)
    dhid = -jnp.einsum('the,hfe->thf', masked, down_b)
    dgate = (dhid * upper * slope).astype(jnp.bfloat16).astype(jnp.float32)
    dup = (dhid * act).astype(jnp.bfloat16).astype(jnp.float32)
    grad_gate = jnp.einsum('thd,thf->hdf', keys, dgate)
    grad_up = jnp.einsum('thd,thf->hdf', keys, dup)
    grad_down = -jnp.einsum('the,thf->hef', masked, hidden)
    grads = jnp.concatenate([grad_gate, grad_up, grad_down], axis=0)
    norms = jnp.sqrt(lax.optimization_barrier(jnp.sum(grads * grads, axis=(1, 2))))
    start = (grads / (norms + 1e-07)[:, None, None]).astype(jnp.bfloat16)
    ortho = newton(start)
    stacked = jnp.concatenate([w_gate, w_up, jnp.transpose(w_down, (0, 2, 1))], axis=0)
    fresh = (stacked - step_size * ortho.astype(jnp.float32)).astype(jnp.bfloat16).astype(jnp.float32)
    gate2 = jnp.einsum('thd,hdf->thf', query, fresh[:HEADS])
    upper2 = jnp.einsum('thd,hdf->thf', query, fresh[HEADS:2 * HEADS])
    hidden2 = (jax.nn.silu(gate2) * upper2).astype(jnp.bfloat16).astype(jnp.float32)
    result = jnp.einsum('thf,hef->the', hidden2, fresh[2 * HEADS:])
    return result.reshape(TOKENS, D).astype(jnp.bfloat16)
```

```python
import functools

import jax
import jax.numpy as jnp
from jax import lax
from jax.experimental import pallas as pl
from jax.experimental.pallas import tpu as pltpu
from jax.sharding import PartitionSpec as P

VIEWS = 16
NS_STEPS = 5
BF16 = jnp.bfloat16
F32 = jnp.float32
VMEM_LIMIT = 40 * 1024 * 1024

coef_a = 3.4445
coef_b = -4.775
coef_c = 2.0315
step_size = 0.8


def mm(a, b, dims):
    return lax.dot_general(a, b, (dims, ((), ())), preferred_element_type=F32)


NN = ((1,), (0,))
NT = ((1,), (1,))
TN = ((0,), (0,))


def project_kernel(plain, flag_ref, tokens_ref, weight_ref, out_ref):
    head_dim = out_ref.shape[2]
    scale = jnp.where(pl.program_id(0) >= plain, flag_ref[0], 1).astype(F32)
    part = mm(tokens_ref[...], weight_ref[...], NN).astype(BF16)
    part = (part.astype(F32) * scale).astype(BF16)
    for head in range(out_ref.shape[0]):
        out_ref[head] = part[:, head * head_dim : (head + 1) * head_dim]


def project(tokens, weight, flag, first, blocks, plain, head_dim):
    rows, width = tokens.shape
    pair = 2
    return pl.pallas_call(
        functools.partial(project_kernel, plain),
        out_shape=jax.ShapeDtypeStruct((blocks * pair, rows, head_dim), BF16),
        grid_spec=pltpu.PrefetchScalarGridSpec(
            num_scalar_prefetch=1,
            grid=(blocks,),
            in_specs=[
                pl.BlockSpec((rows, width), lambda j, flag: (0, 0)),
                pl.BlockSpec((width, pair * head_dim), lambda j, flag: (0, first + j)),
            ],
            out_specs=pl.BlockSpec((pair, rows, head_dim), lambda j, flag: (j, 0, 0)),
        ),
        compiler_params=pltpu.CompilerParams(vmem_limit_bytes=VMEM_LIMIT),
        cost_estimate=pl.CostEstimate(
            flops=2 * rows * width * blocks * pair * head_dim,
            bytes_accessed=2 * width * (rows + blocks * pair * head_dim),
            transcendentals=0,
        ),
    )(flag, tokens, weight)


def grad_kernel(chunk, ids_ref, k_ref, v_ref, gate_ref, up_ref, down_ref, keep_ref, give_ref, up_out_ref):
    core = ids_ref[1]
    rows = k_ref.shape[1]
    gate_b = gate_ref[0].astype(BF16)
    up_b = up_ref[0].astype(BF16)
    down_b = down_ref[0].astype(BF16)
    totals = [None, None, None]
    for start in range(0, rows, chunk):
        k = k_ref[0, pl.ds(start, chunk), :]
        v = v_ref[0, pl.ds(start, chunk), :]
        gate = mm(k, gate_b, NN)
        upper = mm(k, up_b, NN)
        dhid = -mm(v, down_b, NT)
        sig = jax.nn.sigmoid(gate)
        act = gate * sig
        hidden = (act * upper).astype(BF16)
        dgate = (dhid * upper * (sig * (1.0 + gate * (1.0 - sig)))).astype(BF16)
        dup = (dhid * act).astype(BF16)
        parts = [mm(k, dgate, TN), mm(k, dup, TN), -mm(v, hidden, TN)]
        totals = [p if t is None else t + p for t, p in zip(totals, parts)]
    gate_g, up_g, down_g = [t.astype(BF16) for t in totals]
    up_out_ref[...] = up_g

    @pl.when(core == 0)
    def _():
        keep_ref[...] = gate_g
        give_ref[...] = down_g

    @pl.when(core != 0)
    def _():
        keep_ref[...] = down_g
        give_ref[...] = gate_g


def gradients(ids, kv, w_gate, w_up, w_down):
    heads, head_dim, hidden = w_gate.shape
    rows = kv.shape[1]
    whole = pl.BlockSpec((head_dim, hidden), lambda i, ids: (0, 0))
    shape = jax.ShapeDtypeStruct((head_dim, hidden), BF16)
    return pl.pallas_call(
        functools.partial(grad_kernel, rows // 4),
        out_shape=[shape] * 3,
        grid_spec=pltpu.PrefetchScalarGridSpec(
            num_scalar_prefetch=1,
            grid=(1,),
            in_specs=[
                pl.BlockSpec((1, rows, head_dim), lambda i, ids: (ids[0], 0, 0)),
                pl.BlockSpec((1, rows, head_dim), lambda i, ids: (heads + ids[0], 0, 0)),
                pl.BlockSpec((1, head_dim, hidden), lambda i, ids: (ids[0], 0, 0)),
                pl.BlockSpec((1, head_dim, hidden), lambda i, ids: (ids[0], 0, 0)),
                pl.BlockSpec((1, hidden, head_dim), lambda i, ids: (ids[0], 0, 0)),
            ],
            out_specs=[whole] * 3,
        ),
        compiler_params=pltpu.CompilerParams(vmem_limit_bytes=VMEM_LIMIT),
        cost_estimate=pl.CostEstimate(
            flops=12 * rows * head_dim * hidden,
            bytes_accessed=12 * head_dim * hidden + 4 * rows * head_dim,
            transcendentals=rows * hidden,
        ),
    )(ids, kv, kv, w_gate, w_up, w_down)


def newton_kernel(a0_ref, b0_ref, a1_ref, b1_ref, base_ref, out0_ref, out1_ref):
    iterates = []
    for a_ref, b_ref in ((a0_ref, b0_ref), (a1_ref, b1_ref)):
        total = a_ref[...].astype(F32) + b_ref[...].astype(F32)
        norm = jnp.sqrt(jnp.sum(total * total))
        iterates.append((total / (norm + 1e-07)).astype(BF16))
    for step in range(NS_STEPS):
        grams = [mm(x, x, NT).astype(BF16) for x in iterates]
        squares = [mm(g, g, NN) for g in grams]
        mixers = [(coef_b * g.astype(F32) + coef_c * s).astype(BF16) for g, s in zip(grams, squares)]
        moved = [mm(m, x, NN) for m, x in zip(mixers, iterates)]
        iterates = [(coef_a * x.astype(F32) + y).astype(BF16) for x, y in zip(iterates, moved)]
    for slot, (x, out_ref) in enumerate(zip(iterates, (out0_ref, out1_ref))):
        out_ref[...] = (base_ref[slot] - step_size * x.astype(F32)).astype(BF16)


def newton(a0, b0, a1, b1, base):
    head_dim, hidden = a0.shape
    shape = jax.ShapeDtypeStruct((head_dim, hidden), BF16)
    return pl.pallas_call(
        newton_kernel,
        out_shape=[shape] * 2,
        compiler_params=pltpu.CompilerParams(vmem_limit_bytes=VMEM_LIMIT),
        cost_estimate=pl.CostEstimate(
            flops=2 * NS_STEPS * 2 * head_dim * head_dim * (2 * hidden + head_dim),
            bytes_accessed=20 * head_dim * hidden,
            transcendentals=0,
        ),
    )(a0, b0, a1, b1, base)


def apply_kernel(ids_ref, q_ref, s0_ref, s1_ref, x0_ref, x1_ref, out_ref):
    even = ids_ref[1] == 0
    gate_b = jnp.where(even, s0_ref[...], x0_ref[...])
    up_b = jnp.where(even, s1_ref[...], x1_ref[...])
    down_b = jnp.where(even, x0_ref[...], s0_ref[...])
    q = q_ref[0]
    gate = mm(q, gate_b, NN)
    upper = mm(q, up_b, NN)
    hidden = (gate * jax.nn.sigmoid(gate) * upper).astype(BF16)
    out_ref[...] = mm(hidden, down_b, NT).astype(BF16)


def apply(ids, q, s0, s1, x0, x1):
    heads, rows, head_dim = q.shape
    hidden = s0.shape[1]
    whole = pl.BlockSpec((head_dim, hidden), lambda i, ids: (0, 0))
    return pl.pallas_call(
        apply_kernel,
        out_shape=jax.ShapeDtypeStruct((rows, head_dim), BF16),
        grid_spec=pltpu.PrefetchScalarGridSpec(
            num_scalar_prefetch=1,
            grid=(1,),
            in_specs=[pl.BlockSpec((1, rows, head_dim), lambda i, ids: (ids[0], 0, 0))] + [whole] * 4,
            out_specs=pl.BlockSpec((rows, head_dim), lambda i, ids: (0, 0)),
        ),
        compiler_params=pltpu.CompilerParams(vmem_limit_bytes=VMEM_LIMIT),
        cost_estimate=pl.CostEstimate(
            flops=6 * rows * head_dim * hidden,
            bytes_accessed=8 * head_dim * hidden + 4 * rows * head_dim,
            transcendentals=rows * hidden,
        ),
    )(ids, q, s0, s1, x0, x1)


def join_kernel(own_ref, *refs):
    *pieces, out_ref = refs
    own = own_ref[0]
    head_dim = pieces[0].shape[1]
    for case in range(4):

        @pl.when(own == case)
        def _():
            for head in range(4):
                out_ref[:, head * head_dim : (head + 1) * head_dim] = pieces[head ^ case][...]


def join(own, pieces):
    rows, head_dim = pieces[0].shape
    return pl.pallas_call(
        join_kernel,
        out_shape=jax.ShapeDtypeStruct((rows, 4 * head_dim), BF16),
        in_specs=[pl.BlockSpec(memory_space=pltpu.SMEM)] + [pl.BlockSpec(memory_space=pltpu.VMEM)] * 4,
        compiler_params=pltpu.CompilerParams(vmem_limit_bytes=VMEM_LIMIT),
        cost_estimate=pl.CostEstimate(flops=0, bytes_accessed=16 * rows * head_dim, transcendentals=0),
    )(own, *pieces)


def add(*arrays):
    return sum(a.astype(F32) for a in arrays).astype(BF16)


def shards(tokens, qkv_weight, w_gate, w_up, w_down, view_kind):
    rows, width = tokens.shape
    heads, head_dim, hidden = w_gate.shape
    groups = lax.axis_size("tok")
    place = lax.axis_index("tok")
    core = place % 2
    own = (place // 2) % heads
    view_rows = rows * groups // VIEWS
    owner = place * rows // view_rows
    flag = jnp.sum(jnp.where(jnp.arange(VIEWS, dtype=jnp.int32) == owner, view_kind, 0)).reshape(1)

    def exchange(x, bits, parity=None):
        pairs = [(i, i ^ bits) for i in range(groups) if parity is None or i % 2 == parity]
        return lax.ppermute(x, "tok", pairs)

    kv = project(tokens, qkv_weight, flag, 2, 4, 2, head_dim)

    sums = [[], []]
    for far in (3, 1, 2, 0):
        ids = jnp.stack([own ^ far, core]).astype(jnp.int32)
        keep, give, upper = gradients(ids, kv, w_gate, w_up, w_down)
        slot0 = add(keep, exchange(give, 1))
        slot1 = add(upper, exchange(upper, 1, 1))
        if far:
            slot0 = exchange(slot0, 2 * far)
            slot1 = exchange(slot1, 2 * far, 0)
        sums[0].append(slot0)
        sums[1].append(slot1)
    query = project(tokens, qkv_weight, flag, 0, 2, 2, head_dim)

    slot0, slot1 = add(*sums[0]), add(*sums[1])
    bits = 8
    while bits < groups // 2:
        slot0, slot1 = add(slot0, exchange(slot0, bits)), add(slot1, exchange(slot1, bits, 0))
        bits *= 2
    other0, other1 = exchange(slot0, bits), exchange(slot1, bits, 0)

    mine = lambda w: lax.dynamic_index_in_dim(w, own, 0, keepdims=False)
    base = jnp.stack([jnp.where(core == 0, mine(w_gate), mine(w_down).T), mine(w_up)])
    fresh0, fresh1 = newton(slot0, other0, slot1, other1, base)

    pieces = []
    for far in range(heads):
        here0 = exchange(fresh0, 2 * far) if far else fresh0
        here1 = exchange(fresh1, 2 * far, 0) if far else fresh1
        there0, there1 = exchange(here0, 1), exchange(here1, 1, 0)
        ids = jnp.stack([own ^ far, core]).astype(jnp.int32)
        pieces.append(apply(ids, query, here0, here1, there0, there1))
    return join(own.reshape(1).astype(jnp.int32), pieces)


def solution(mesh):
    placed = (P(("scene", "tok"), None), P(), P(), P(), P(), P("scene"))
    return jax.shard_map(
        shards, mesh=mesh, in_specs=placed, out_specs=P(("scene", "tok"), None), check_vma=False
    )
```

```python
import functools

import jax
import jax.numpy as jnp
from jax import lax
from jax.experimental import pallas as pl
from jax.experimental.pallas import tpu as pltpu
from jax.sharding import PartitionSpec as P

VIEWS = 16
NS_STEPS = 5
BF16 = jnp.bfloat16
F32 = jnp.float32
K1_LIMIT = 62
SMALL_LIMIT = 24

coef_a = 3.4445
coef_b = -4.775
coef_c = 2.0315
step_size = 0.8


def mm(a, b, dims):
    return lax.dot_general(a, b, (dims, ((), ())), preferred_element_type=F32)


NN = ((1,), (0,))
NT = ((1,), (1,))
TN = ((0,), (0,))


def grad_kernel(ids_ref, view_ref, tok_hbm, qkv_hbm, gate_hbm, up_hbm, down_hbm, keep_ref, give_ref, tok, wkv, fast, kv, both_w, down_w, sems):
    own, core, owner = ids_ref[0], ids_ref[1], ids_ref[2]
    rows, width = tok.shape
    head_dim = kv.shape[3]
    hidden = down_w.shape[2]
    heads = gate_hbm.shape[0]
    span = 2 * head_dim
    pairs = heads // 2
    half = head_dim // 2
    count = iter(range(3 + 2 * pairs + 3 * heads))

    def fetch(source, target):
        copy = pltpu.make_async_copy(source, target, sems.at[next(count)])
        copy.start()
        return copy

    tok_copy = fetch(tok_hbm, tok)
    kv_copies, fast_copies = [], []
    for pair in range(pairs):
        kv_copies.append([
            fetch(qkv_hbm.at[:, (1 + which) * width + pair * span : (1 + which) * width + (pair + 1) * span], wkv.at[pair, which])
            for which in range(2)
        ])
        for head in (2 * pair, 2 * pair + 1):
            fast_copies.append([fetch(ref.at[head], fast.at[head, i]) for i, ref in enumerate((gate_hbm, up_hbm, down_hbm))])

    flag = view_ref[owner].astype(F32)
    tok_copy.wait()
    for pair in range(pairs):
        for which in range(2):
            kv_copies[pair][which].wait()
            part = mm(tok[...], wkv[pair, which], NN).astype(BF16)
            if which == 1:
                part = (part.astype(F32) * flag).astype(BF16)
            kv[which, 0] = part[:, :head_dim]
            kv[which, 1] = part[:, head_dim:]
        for inner in range(2):
            head = 2 * pair + inner
            for copy in fast_copies[head]:
                copy.wait()
            both_w[inner, :, :hidden] = fast[head, 0].astype(BF16)
            both_w[inner, :, hidden:] = fast[head, 1].astype(BF16)
            down_w[inner] = fast[head, 2].astype(BF16)
            both_sum = down_sum = None
            chunk = rows // 2
            for start in range(0, rows, chunk):
                k = kv[0, inner, start : start + chunk, :]
                v = kv[1, inner, start : start + chunk, :]
                both = mm(k, both_w[inner], NN)
                dhid = -mm(v, down_w[inner], NN)
                gate, upper = both[:, :hidden], both[:, hidden:]
                sig = jax.nn.sigmoid(gate)
                act = gate * sig
                hid = (act * upper).astype(BF16)
                dgate = (dhid * upper * (sig * (1.0 + gate * (1.0 - sig)))).astype(BF16)
                dup = (dhid * act).astype(BF16)
                both_part = mm(k, jnp.concatenate([dgate, dup], axis=1), TN)
                down_part = mm(v, hid, TN)
                both_sum = both_part if both_sum is None else both_sum + both_part
                down_sum = down_part if down_sum is None else down_sum + down_part
            gate_g = both_sum[:, :hidden].astype(BF16)
            up_g = both_sum[:, hidden:].astype(BF16)
            down_g = (-down_sum).astype(BF16)
            slot = own ^ head

            @pl.when(core == 0)
            def _():
                keep_ref[slot, :head_dim] = gate_g
                keep_ref[slot, head_dim:] = up_g[:half]
                give_ref[slot, :head_dim] = down_g
                give_ref[slot, head_dim:] = up_g[half:]

            @pl.when(core != 0)
            def _():
                keep_ref[slot, :head_dim] = down_g
                keep_ref[slot, head_dim:] = up_g[half:]
                give_ref[slot, :head_dim] = gate_g
                give_ref[slot, head_dim:] = up_g[:half]


def gradients(ids, view_kind, tokens, qkv_weight, w_gate, w_up, w_down_t):
    rows, width = tokens.shape
    heads, head_dim, hidden = w_gate.shape
    pairs = heads // 2
    smem, vmem, hbm = (pl.BlockSpec(memory_space=s) for s in (pltpu.SMEM, pltpu.VMEM, pl.ANY))
    shape = jax.ShapeDtypeStruct((heads, head_dim * 3 // 2, hidden), BF16)
    return pl.pallas_call(
        grad_kernel,
        out_shape=[shape] * 2,
        in_specs=[smem] * 2 + [hbm] * 5,
        out_specs=[vmem] * 2,
        scratch_shapes=[
            pltpu.VMEM((rows, width), BF16),
            pltpu.VMEM((pairs, 2, width, 2 * head_dim), BF16),
            pltpu.VMEM((heads, 3, head_dim, hidden), F32),
            pltpu.VMEM((2, 2, rows, head_dim), BF16),
            pltpu.VMEM((2, head_dim, 2 * hidden), BF16),
            pltpu.VMEM((2, head_dim, hidden), BF16),
            pltpu.SemaphoreType.DMA((1 + 2 * pairs + 3 * heads,)),
        ],
        compiler_params=pltpu.CompilerParams(vmem_limit_bytes=K1_LIMIT * 1024 * 1024),
        cost_estimate=pl.CostEstimate(
            flops=4 * rows * width * width + 12 * heads * rows * head_dim * hidden,
            bytes_accessed=2 * rows * width + 4 * width * width + 12 * heads * head_dim * hidden,
            transcendentals=heads * rows * hidden,
        ),
        name="gradients",
    )(ids, view_kind, tokens, qkv_weight, w_gate, w_up, w_down_t)


def small(kernel, shapes, operands, smem=0, flops=0, nbytes=0, name=None):
    specs = [pl.BlockSpec(memory_space=pltpu.SMEM)] * smem + [pl.BlockSpec(memory_space=pltpu.VMEM)] * (len(operands) - smem)
    return pl.pallas_call(
        kernel,
        out_shape=shapes,
        in_specs=specs,
        compiler_params=pltpu.CompilerParams(vmem_limit_bytes=SMALL_LIMIT * 1024 * 1024),
        cost_estimate=pl.CostEstimate(flops=flops, bytes_accessed=nbytes, transcendentals=0),
        name=name,
    )(*operands)


def query_kernel(tokens_ref, weight_ref, out_ref):
    heads, _, head_dim = out_ref.shape
    part = mm(tokens_ref[...], weight_ref[...], NN).astype(BF16)
    for head in range(heads):
        out_ref[head] = part[:, head * head_dim : (head + 1) * head_dim]


def project_query(tokens, weight, heads):
    rows, width = tokens.shape
    return pl.pallas_call(
        query_kernel,
        out_shape=jax.ShapeDtypeStruct((heads, rows, width // heads), BF16),
        grid=(1,),
        in_specs=[pl.BlockSpec((rows, width), lambda i: (0, 0)), pl.BlockSpec((width, width), lambda i: (0, 0))],
        out_specs=pl.BlockSpec((heads, rows, width // heads), lambda i: (0, 0, 0)),
        compiler_params=pltpu.CompilerParams(vmem_limit_bytes=SMALL_LIMIT * 1024 * 1024),
        cost_estimate=pl.CostEstimate(flops=2 * rows * width * width, bytes_accessed=4 * width * (rows + width), transcendentals=0),
        name="query",
    )(tokens, weight)


def pair_sum_kernel(keep_ref, got_ref, *out_refs):
    for slot, out_ref in enumerate(out_refs):
        out_ref[...] = (keep_ref[slot].astype(F32) + got_ref[slot].astype(F32)).astype(BF16)


def sum_kernel(*refs):
    *parts, out_ref = refs
    total = parts[0][...].astype(F32)
    for part in parts[1:]:
        total = total + part[...].astype(F32)
    out_ref[...] = total.astype(BF16)


def newton_kernel(core_ref, mine_ref, other_ref, half_ref, got_ref, base_ref, base_half_ref, out_ref):
    head_dim = base_ref.shape[0]
    half = half_ref.shape[0]
    even = core_ref[0] == 0
    first = mine_ref[:head_dim].astype(F32) + other_ref[:head_dim].astype(F32)
    a, b = half_ref[...], got_ref[...]
    second = jnp.concatenate([jnp.where(even, a, b), jnp.where(even, b, a)], axis=0).astype(F32)
    iterates = []
    for total in (first, second):
        norm = jnp.sqrt(jnp.sum(total * total))
        iterates.append((total / (norm + 1e-07)).astype(BF16))
    for step in range(NS_STEPS):
        grams = [mm(x, x, NT).astype(BF16) for x in iterates]
        squares = [mm(g, g, NN) for g in grams]
        mixers = [(coef_b * g.astype(F32) + coef_c * s).astype(BF16) for g, s in zip(grams, squares)]
        moved = [mm(m, x, NN) for m, x in zip(mixers, iterates)]
        iterates = [(coef_a * x.astype(F32) + y).astype(BF16) for x, y in zip(iterates, moved)]
    first, second = [x.astype(F32) for x in iterates]
    out_ref[:head_dim] = (base_ref[...] - step_size * first).astype(BF16)
    second = jnp.where(even, second[:half], second[half:])
    out_ref[head_dim:] = (base_half_ref[...] - step_size * second).astype(BF16)


def head_output(even, q, here_ref, there_ref):
    head_dim = q.shape[1]
    here, there = here_ref[...], there_ref[...]
    a, b = jnp.where(even, here, there), jnp.where(even, there, here)
    up_b = jnp.concatenate([a[head_dim:], b[head_dim:]], axis=0)
    gate = mm(q, a[:head_dim], NN)
    upper = mm(q, up_b, NN)
    hidden = (gate * jax.nn.sigmoid(gate) * upper).astype(BF16)
    return mm(hidden, b[:head_dim], NT).astype(BF16)


def apply_kernel(ids_ref, q_ref, here_ref, there_ref, out_ref):
    out_ref[...] = head_output(ids_ref[1] == 0, q_ref[ids_ref[0]], here_ref, there_ref)


def finish_kernel(ids_ref, q_ref, here_ref, there_ref, *refs):
    *pieces, out_ref = refs
    heads, _, head_dim = q_ref.shape
    last = ids_ref[0]
    own = last ^ (heads - 1)
    piece = head_output(ids_ref[1] == 0, q_ref[last], here_ref, there_ref)
    for case in range(heads):

        @pl.when(own == case)
        def _():
            for head in range(heads):
                far = head ^ case
                out_ref[:, head * head_dim : (head + 1) * head_dim] = piece if far == heads - 1 else pieces[far][...]


def shards(tokens, qkv_weight, w_gate, w_up, w_down, view_kind):
    rows, width = tokens.shape
    heads, head_dim, hidden = w_gate.shape
    groups = lax.axis_size("tok")
    place = lax.axis_index("tok")
    core = place % 2
    own = (place // 2) % heads
    view_rows = rows * groups // VIEWS
    owner = place * rows // view_rows
    w_down_t = jnp.transpose(w_down, (0, 2, 1))
    block = jax.ShapeDtypeStruct((head_dim * 3 // 2, hidden), BF16)
    half = head_dim // 2

    def exchange(x, bits):
        return lax.ppermute(x, "tok", [(i, i ^ bits) for i in range(groups)])

    ids = jnp.stack([own, core, owner]).astype(jnp.int32)
    keep, give = gradients(ids, view_kind, tokens, qkv_weight, w_gate, w_up, w_down_t)
    got = exchange(give, 1)
    sums = small(pair_sum_kernel, [block] * heads, (keep, got), name="pair_sum", nbytes=9 * keep.size)
    arrived = [exchange(sums[far], 2 * far) for far in (3, 1, 2)]
    query = project_query(tokens, qkv_weight, heads)

    mine = lambda w: lax.dynamic_index_in_dim(w, own, 0, keepdims=False)
    base = jnp.where(core == 0, mine(w_gate), mine(w_down_t))
    base_half = lax.dynamic_slice_in_dim(mine(w_up), core * half, half, 0)

    total = small(sum_kernel, block, (sums[0], *arrived), name="plane_sum", nbytes=10 * block.size)
    bits = 2 * heads
    while bits < groups // 2:
        total = small(sum_kernel, block, (total, exchange(total, bits)), name="line_sum", nbytes=6 * block.size)
        bits *= 2
    other = exchange(total, bits)
    up_half = total[head_dim:].astype(F32) + other[head_dim:].astype(F32)
    up_half = up_half.astype(BF16)
    got_half = exchange(up_half, 1)
    fresh = small(
        newton_kernel, block, (core.reshape(1), total, other, up_half, got_half, base, base_half), smem=1,
        flops=2 * NS_STEPS * 2 * head_dim * head_dim * (2 * hidden + head_dim), nbytes=12 * block.size, name="newton",
    )

    here = [fresh] + [exchange(fresh, 2 * far) for far in range(1, heads)]
    there = [exchange(h, 1) for h in here]
    pieces = []
    cost = dict(flops=6 * rows * head_dim * hidden, nbytes=4 * block.size + 4 * rows * head_dim)
    for far in range(heads):
        ids = jnp.stack([own ^ far, core]).astype(jnp.int32)
        args = (ids, query, here[far], there[far])
        if far < heads - 1:
            piece = jax.ShapeDtypeStruct((rows, head_dim), BF16)
            pieces.append(small(apply_kernel, piece, args, smem=1, name="apply", **cost))
    whole = jax.ShapeDtypeStruct((rows, width), BF16)
    return small(finish_kernel, whole, (*args, *pieces), smem=1, name="finish", **cost)


def solution(mesh):
    placed = (P(("scene", "tok"), None), P(), P(), P(), P(), P("scene"))
    return jax.shard_map(
        shards, mesh=mesh, in_specs=placed, out_specs=P(("scene", "tok"), None), check_vma=False
    )
```

```python
import functools

import jax
import jax.numpy as jnp
from jax import lax
from jax.experimental import pallas as pl
from jax.experimental.pallas import tpu as pltpu
from jax.sharding import PartitionSpec as P

VIEWS = 16
NS_STEPS = 5
BF16 = jnp.bfloat16
F32 = jnp.float32
K1_LIMIT = 40
SMALL_LIMIT = 24

coef_a = 3.4445
coef_b = -4.775
coef_c = 2.0315
step_size = 0.8


def mm(a, b, dims):
    return lax.dot_general(a, b, (dims, ((), ())), preferred_element_type=F32)


NN = ((1,), (0,))
NT = ((1,), (1,))
TN = ((0,), (0,))


def position(heads):
    place = lax.axis_index("tok")
    return lax.rem(lax.div(place, 2), heads), lax.rem(place, 2)


def grad_kernel(
    view_hbm, tok_hbm, qkv_hbm, gate_hbm, up_hbm, down_hbm, keep_ref, give_ref, view, tok, wkv, fast, kv, both_w, down_w, sems
):
    rows, width = tok.shape
    heads, head_dim = kv.shape[1], kv.shape[3]
    hidden = down_w.shape[2]
    half = head_dim // 2
    own, core = position(heads)
    owner = lax.div(lax.axis_index("tok") * rows, rows * lax.axis_size("tok") // VIEWS)
    count = iter(range(4 + 3 * heads))

    def fetch(source, target):
        copy = pltpu.make_async_copy(source, target, sems.at[next(count)])
        copy.start()
        return copy

    tok_copy = fetch(tok_hbm, tok)
    kv_copies = [fetch(qkv_hbm.at[:, (1 + which) * width : (2 + which) * width], wkv.at[which]) for which in range(2)]
    view_copy = fetch(view_hbm, view)
    fast_copies = [
        fetch(ref.at[head], fast.at[head, i]) for head in range(heads) for i, ref in enumerate((gate_hbm, up_hbm, down_hbm))
    ]
    tok_copy.wait()
    view_copy.wait()
    flag = view[owner].astype(F32)
    for which in range(2):
        kv_copies[which].wait()
        for pair in range(heads // 2):
            columns = slice(2 * pair * head_dim, (2 * pair + 2) * head_dim)
            part = mm(tok[...], wkv[which, :, columns], NN).astype(BF16)
            if which == 1:
                part = (part.astype(F32) * flag).astype(BF16)
            kv[which, 2 * pair] = part[:, :head_dim]
            kv[which, 2 * pair + 1] = part[:, head_dim:]
    for copy in fast_copies:
        copy.wait()
    for head in range(heads):
        both_w[head, :, :hidden] = fast[head, 0].astype(BF16)
        both_w[head, :, hidden:] = fast[head, 1].astype(BF16)
        down_w[head] = fast[head, 2].astype(BF16)
    even = core == 0
    chunk = rows // 2
    for head in range(heads):
        both_sum = down_sum = None
        for start in range(0, rows, chunk):
            k = kv[0, head, start : start + chunk, :]
            v = kv[1, head, start : start + chunk, :]
            both = mm(k, both_w[head], NN)
            dhid = -mm(v, down_w[head], NN)
            gate, upper = both[:, :hidden], both[:, hidden:]
            sig = jax.nn.sigmoid(gate)
            act = gate * sig
            hid = (act * upper).astype(BF16)
            dgate = (dhid * upper * (sig * (1.0 + gate * (1.0 - sig)))).astype(BF16)
            dup = (dhid * act).astype(BF16)
            both_part = mm(k, jnp.concatenate([dgate, dup], axis=1), TN)
            down_part = mm(v, hid, TN)
            both_sum = both_part if both_sum is None else both_sum + both_part
            down_sum = down_part if down_sum is None else down_sum + down_part
        gate_g = both_sum[:, :hidden].astype(BF16)
        up_g = both_sum[:, hidden:].astype(BF16)
        down_g = (-down_sum).astype(BF16)
        slot = own ^ head
        keep_ref[slot, :head_dim] = jnp.where(even, gate_g, down_g)
        give_ref[slot, :head_dim] = jnp.where(even, down_g, gate_g)
        keep_ref[slot, head_dim:] = jnp.where(even, up_g[:half], up_g[half:])
        give_ref[slot, head_dim:] = jnp.where(even, up_g[half:], up_g[:half])


def gradients(view_kind, tokens, qkv_weight, w_gate, w_up, w_down_t):
    rows, width = tokens.shape
    heads, head_dim, hidden = w_gate.shape
    args = [pltpu.with_memory_space_constraint(x, pltpu.HBM) for x in (view_kind, tokens, qkv_weight, w_gate, w_up, w_down_t)]
    shape = pltpu.VMEM((heads, head_dim * 3 // 2, hidden), BF16)
    return pl.pallas_call(
        grad_kernel,
        out_shape=[shape] * 2,
        in_specs=[pl.BlockSpec(memory_space=pl.ANY)] * 6,
        out_specs=[pl.BlockSpec(memory_space=pltpu.VMEM)] * 2,
        scratch_shapes=[
            pltpu.SMEM(view_kind.shape, jnp.int32),
            pltpu.VMEM((rows, width), BF16),
            pltpu.VMEM((2, width, width), BF16),
            pltpu.VMEM((heads, 3, head_dim, hidden), F32),
            pltpu.VMEM((2, heads, rows, head_dim), BF16),
            pltpu.VMEM((heads, head_dim, 2 * hidden), BF16),
            pltpu.VMEM((heads, head_dim, hidden), BF16),
            pltpu.SemaphoreType.DMA((4 + 3 * heads,)),
        ],
        compiler_params=pltpu.CompilerParams(vmem_limit_bytes=K1_LIMIT * 1024 * 1024),
        cost_estimate=pl.CostEstimate(
            flops=4 * rows * width * width + 12 * heads * rows * head_dim * hidden,
            bytes_accessed=2 * rows * width + 4 * width * width + 12 * heads * head_dim * hidden,
            transcendentals=heads * rows * hidden,
        ),
        name="gradients",
    )(*args)


def small(kernel, shapes, operands, nbytes, name):
    specs = [pl.BlockSpec(memory_space=pltpu.VMEM)] * len(operands)
    operands = [pltpu.with_memory_space_constraint(x, pltpu.VMEM) for x in operands]
    return pl.pallas_call(
        kernel,
        out_shape=shapes,
        in_specs=specs,
        compiler_params=pltpu.CompilerParams(vmem_limit_bytes=SMALL_LIMIT * 1024 * 1024),
        cost_estimate=pl.CostEstimate(flops=0, bytes_accessed=nbytes, transcendentals=0),
        name=name,
    )(*operands)


def query_kernel(tokens_ref, weight_ref, out_ref):
    heads, _, head_dim = out_ref.shape
    part = mm(tokens_ref[...], weight_ref[...], NN).astype(BF16)
    for head in range(heads):
        out_ref[head] = part[:, head * head_dim : (head + 1) * head_dim]


def project_query(tokens, weight, heads):
    rows, width = tokens.shape
    return pl.pallas_call(
        query_kernel,
        out_shape=pltpu.VMEM((heads, rows, width // heads), BF16),
        grid=(1,),
        in_specs=[pl.BlockSpec((rows, width), lambda i: (0, 0)), pl.BlockSpec((width, width), lambda i: (0, 0))],
        out_specs=pl.BlockSpec((heads, rows, width // heads), lambda i: (0, 0, 0)),
        compiler_params=pltpu.CompilerParams(vmem_limit_bytes=SMALL_LIMIT * 1024 * 1024),
        cost_estimate=pl.CostEstimate(flops=2 * rows * width * width, bytes_accessed=4 * width * (rows + width), transcendentals=0),
        name="query",
    )(*(pltpu.with_memory_space_constraint(x, pltpu.HBM) for x in (tokens, weight)))


def pair_sum_kernel(keep_ref, got_ref, *out_refs):
    heads = len(out_refs) // 2
    main = out_refs[0].shape[0]
    for slot in range(heads):
        total = (keep_ref[slot].astype(F32) + got_ref[slot].astype(F32)).astype(BF16)
        out_refs[slot][...] = total[:main]
        out_refs[heads + slot][...] = total[main:]


def sum_kernel(*refs):
    *parts, out_ref = refs
    total = parts[0][...].astype(F32)
    for part in parts[1:]:
        total = total + part[...].astype(F32)
    out_ref[...] = total.astype(BF16)


def stepped(total, base):
    norm = jnp.sqrt(jnp.sum(total * total))
    x = (total / (norm + 1e-07)).astype(BF16)
    for step in range(NS_STEPS):
        gram = mm(x, x, NT).astype(BF16)
        square = mm(gram, gram, NN)
        mixer = (coef_b * gram.astype(F32) + coef_c * square).astype(BF16)
        x = (coef_a * x.astype(F32) + mm(mixer, x, NN)).astype(BF16)
    return (base - step_size * x.astype(F32)).astype(BF16)


def newton_kernel(mine_ref, other_ref, base_ref, out_ref):
    out_ref[...] = stepped(mine_ref[...].astype(F32) + other_ref[...].astype(F32), base_ref[...])


def newton_up_kernel(heads, mine_ref, got_ref, base_ref, out_ref, half_ref):
    half = mine_ref.shape[0]
    even = position(heads)[1] == 0
    a, b = mine_ref[...], got_ref[...]
    total = jnp.concatenate([jnp.where(even, a, b), jnp.where(even, b, a)], axis=0).astype(F32)
    fresh = stepped(total, base_ref[...])
    out_ref[...] = fresh
    half_ref[...] = jnp.where(even, fresh[:half], fresh[half:])


def head_output(even, q, main_ref, main_there_ref, up_refs):
    here, there = main_ref[...], main_there_ref[...]
    gate_b, down_b = jnp.where(even, here, there), jnp.where(even, there, here)
    if len(up_refs) == 1:
        up_b = up_refs[0][...]
    else:
        a, b = up_refs[0][...], up_refs[1][...]
        up_b = jnp.concatenate([jnp.where(even, a, b), jnp.where(even, b, a)], axis=0)
    gate = mm(q, gate_b, NN)
    upper = mm(q, up_b, NN)
    hidden = (gate * jax.nn.sigmoid(gate) * upper).astype(BF16)
    return mm(hidden, down_b, NT).astype(BF16)


def apply_kernel(far, q_ref, main_ref, main_there_ref, *refs):
    *up_refs, out_ref = refs
    own, core = position(q_ref.shape[0])
    out_ref[...] = head_output(core == 0, q_ref[own ^ far], main_ref, main_there_ref, up_refs)


def finish_kernel(q_ref, main_ref, main_there_ref, up_ref, up_there_ref, *refs):
    *pieces, out_ref = refs
    heads, _, head_dim = q_ref.shape
    own, core = position(heads)
    piece = head_output(core == 0, q_ref[own ^ (heads - 1)], main_ref, main_there_ref, (up_ref, up_there_ref))
    for case in range(heads):

        @pl.when(own == case)
        def _():
            for head in range(heads):
                far = head ^ case
                out_ref[:, head * head_dim : (head + 1) * head_dim] = piece if far == heads - 1 else pieces[far][...]


def shards(tokens, qkv_weight, w_gate, w_up, w_down, view_kind):
    rows, width = tokens.shape
    heads, head_dim, hidden = w_gate.shape
    groups = lax.axis_size("tok")
    own, core = position(heads)
    w_down_t = jnp.transpose(w_down, (0, 2, 1))
    half = head_dim // 2
    shape = lambda *dims: pltpu.VMEM(dims, BF16)
    size = head_dim * hidden
    main_block, half_block = shape(head_dim, hidden), shape(half, hidden)
    size = head_dim * hidden

    def exchange(x, bits):
        return lax.ppermute(x, "tok", [(i, i ^ bits) for i in range(groups)])

    keep, give = gradients(view_kind, tokens, qkv_weight, w_gate, w_up, w_down_t)
    got = exchange(give, 1)
    sums = small(pair_sum_kernel, [main_block] * heads + [half_block] * heads, (keep, got), 9 * keep.size, "pair_sum")
    mains, ups = sums[:heads], sums[heads:]
    ups_in = [exchange(ups[far], 2 * far) for far in (1, 2, 3)]
    mains_in = [exchange(mains[far], 2 * far) for far in (1, 2, 3)]
    query = project_query(tokens, qkv_weight, heads)
    base = jnp.where(core == 0, lax.dynamic_index_in_dim(w_gate, own, 0, False), lax.dynamic_index_in_dim(w_down_t, own, 0, False))
    base_up = lax.dynamic_index_in_dim(w_up, own, 0, False)
    mains_in, query, base, base_up = lax.optimization_barrier((mains_in, query, base, base_up))

    def over_line(total, name):
        bits = 2 * heads
        while bits < groups // 2:
            total = small(sum_kernel, shape(*total.shape), (total, exchange(total, bits)), 6 * total.size, name)
            bits *= 2
        return total, exchange(total, bits)

    up_total = small(sum_kernel, half_block, (ups[0], *ups_in), 10 * size, "plane_sum_up")
    up_total, up_other = over_line(up_total, "line_sum_up")
    main_total = small(sum_kernel, main_block, (mains[0], *mains_in), 10 * size, "plane_sum")
    main_total, main_other = over_line(main_total, "line_sum")
    up_half = small(sum_kernel, half_block, (up_total, up_other), 10 * size, "up_sum")
    up_got = exchange(up_half, 1)
    up_fresh, up_out = small(
        functools.partial(newton_up_kernel, heads), [main_block, half_block], (up_half, up_got, base_up), 30 * size, "newton_up"
    )
    ups_here = [exchange(up_out, 2 * far) for far in range(1, heads)]
    ups_there = [exchange(x, 1) for x in ups_here]
    fresh = small(newton_kernel, main_block, (main_total, main_other, base), 30 * size, "newton")

    def apply(far, *args):
        return small(functools.partial(apply_kernel, far), shape(rows, head_dim), (query, *args), 20 * rows * head_dim, "apply")

    here = [exchange(fresh, 2 * far) for far in range(1, heads)]
    pieces = [apply(0, fresh, exchange(fresh, 1), up_fresh)]
    here, pieces = lax.optimization_barrier((here, pieces))
    there = [exchange(x, 1) for x in here]
    for far in range(1, heads - 1):
        pieces.append(apply(far, here[far - 1], there[far - 1], ups_here[far - 1], ups_there[far - 1]))
    args = (query, here[-1], there[-1], ups_here[-1], ups_there[-1], *pieces)
    return small(finish_kernel, jax.ShapeDtypeStruct((rows, width), BF16), args, 20 * rows * head_dim, "finish")


def solution(mesh):
    placed = (P(("scene", "tok"), None), P(), P(), P(), P(), P("scene"))
    return jax.shard_map(
        shards, mesh=mesh, in_specs=placed, out_specs=P(("scene", "tok"), None), check_vma=False
    )
```

```python
import functools

import jax
import jax.numpy as jnp
from jax import lax
from jax.experimental import pallas as pl
from jax.experimental.pallas import tpu as pltpu
from jax.sharding import PartitionSpec as P

VIEWS = 16
NS_STEPS = 5
BF16 = jnp.bfloat16
F32 = jnp.float32
K1_LIMIT = 40
SMALL_LIMIT = 24
FINISH_LOTS = 2

coef_a = 3.4445
coef_b = -4.775
coef_c = 2.0315
step_size = 0.8


def mm(a, b, dims):
    return lax.dot_general(a, b, (dims, ((), ())), preferred_element_type=F32)


NN = ((1,), (0,))
NT = ((1,), (1,))
TN = ((0,), (0,))


def position(heads):
    place = lax.axis_index("tok")
    return lax.rem(lax.div(place, 2), heads), lax.rem(place, 2)


def grad_kernel(
    view_hbm, tok_hbm, qkv_hbm, gate_hbm, up_hbm, down_hbm, keep_ref, give_ref, view, tok, wkv, fast, kv, both_w, down_w, sems
):
    rows, width = tok.shape
    heads, head_dim = kv.shape[1], kv.shape[3]
    hidden = down_w.shape[2]
    half = head_dim // 2
    own, core = position(heads)
    owner = lax.div(lax.axis_index("tok") * rows, rows * lax.axis_size("tok") // VIEWS)
    count = iter(range(4 + 3 * heads))

    def fetch(source, target):
        copy = pltpu.make_async_copy(source, target, sems.at[next(count)])
        copy.start()
        return copy

    tok_copy = fetch(tok_hbm, tok)
    kv_copies = [fetch(qkv_hbm.at[:, (1 + which) * width : (2 + which) * width], wkv.at[which]) for which in range(2)]
    view_copy = fetch(view_hbm, view)
    fast_copies = [
        fetch(ref.at[head], fast.at[head, i]) for head in range(heads) for i, ref in enumerate((gate_hbm, up_hbm, down_hbm))
    ]
    tok_copy.wait()
    view_copy.wait()
    flag = view[owner].astype(F32)
    for which in range(2):
        kv_copies[which].wait()
        for pair in range(heads // 2):
            columns = slice(2 * pair * head_dim, (2 * pair + 2) * head_dim)
            part = mm(tok[...], wkv[which, :, columns], NN).astype(BF16)
            if which == 1:
                part = (part.astype(F32) * flag).astype(BF16)
            kv[which, 2 * pair] = part[:, :head_dim]
            kv[which, 2 * pair + 1] = part[:, head_dim:]
    for copy in fast_copies:
        copy.wait()
    for head in range(heads):
        both_w[head, :, :hidden] = fast[head, 0].astype(BF16)
        both_w[head, :, hidden:] = fast[head, 1].astype(BF16)
        down_w[head] = fast[head, 2].astype(BF16)
    even = core == 0
    chunk = rows // 2
    for head in range(heads):
        both_sum = down_sum = None
        for start in range(0, rows, chunk):
            k = kv[0, head, start : start + chunk, :]
            v = kv[1, head, start : start + chunk, :]
            both = mm(k, both_w[head], NN)
            dhid = -mm(v, down_w[head], NN)
            gate, upper = both[:, :hidden], both[:, hidden:]
            sig = jax.nn.sigmoid(gate)
            act = gate * sig
            hid = (act * upper).astype(BF16)
            dgate = (dhid * upper * (sig * (1.0 + gate * (1.0 - sig)))).astype(BF16)
            dup = (dhid * act).astype(BF16)
            both_part = mm(k, jnp.concatenate([dgate, dup], axis=1), TN)
            down_part = mm(v, hid, TN)
            both_sum = both_part if both_sum is None else both_sum + both_part
            down_sum = down_part if down_sum is None else down_sum + down_part
        gate_g = both_sum[:, :hidden].astype(BF16)
        up_g = both_sum[:, hidden:].astype(BF16)
        down_g = (-down_sum).astype(BF16)
        slot = own ^ head
        keep_ref[slot, :head_dim] = jnp.where(even, gate_g, down_g)
        give_ref[slot, :head_dim] = jnp.where(even, down_g, gate_g)
        keep_ref[slot, head_dim:] = jnp.where(even, up_g[:half], up_g[half:])
        give_ref[slot, head_dim:] = jnp.where(even, up_g[half:], up_g[:half])


def gradients(view_kind, tokens, qkv_weight, w_gate, w_up, w_down_t):
    rows, width = tokens.shape
    heads, head_dim, hidden = w_gate.shape
    args = [pltpu.with_memory_space_constraint(x, pltpu.HBM) for x in (view_kind, tokens, qkv_weight, w_gate, w_up, w_down_t)]
    shape = pltpu.VMEM((heads, head_dim * 3 // 2, hidden), BF16)
    return pl.pallas_call(
        grad_kernel,
        out_shape=[shape] * 2,
        in_specs=[pl.BlockSpec(memory_space=pl.ANY)] * 6,
        out_specs=[pl.BlockSpec(memory_space=pltpu.VMEM)] * 2,
        scratch_shapes=[
            pltpu.SMEM(view_kind.shape, jnp.int32),
            pltpu.VMEM((rows, width), BF16),
            pltpu.VMEM((2, width, width), BF16),
            pltpu.VMEM((heads, 3, head_dim, hidden), F32),
            pltpu.VMEM((2, heads, rows, head_dim), BF16),
            pltpu.VMEM((heads, head_dim, 2 * hidden), BF16),
            pltpu.VMEM((heads, head_dim, hidden), BF16),
            pltpu.SemaphoreType.DMA((4 + 3 * heads,)),
        ],
        compiler_params=pltpu.CompilerParams(vmem_limit_bytes=K1_LIMIT * 1024 * 1024),
        cost_estimate=pl.CostEstimate(
            flops=4 * rows * width * width + 12 * heads * rows * head_dim * hidden,
            bytes_accessed=2 * rows * width + 4 * width * width + 12 * heads * head_dim * hidden,
            transcendentals=heads * rows * hidden,
        ),
        name="gradients",
    )(*args)


def small(kernel, shapes, operands, nbytes, name):
    specs = [pl.BlockSpec(memory_space=pltpu.VMEM)] * len(operands)
    operands = [pltpu.with_memory_space_constraint(x, pltpu.VMEM) for x in operands]
    return pl.pallas_call(
        kernel,
        out_shape=shapes,
        in_specs=specs,
        compiler_params=pltpu.CompilerParams(vmem_limit_bytes=SMALL_LIMIT * 1024 * 1024),
        cost_estimate=pl.CostEstimate(flops=0, bytes_accessed=nbytes, transcendentals=0),
        name=name,
    )(*operands)


def query_kernel(tokens_ref, weight_ref, out_ref):
    heads, _, head_dim = out_ref.shape
    part = mm(tokens_ref[...], weight_ref[...], NN).astype(BF16)
    for head in range(heads):
        out_ref[head] = part[:, head * head_dim : (head + 1) * head_dim]


def project_query(tokens, weight, heads):
    rows, width = tokens.shape
    return pl.pallas_call(
        query_kernel,
        out_shape=pltpu.VMEM((heads, rows, width // heads), BF16),
        grid=(1,),
        in_specs=[pl.BlockSpec((rows, width), lambda i: (0, 0)), pl.BlockSpec((width, width), lambda i: (0, 0))],
        out_specs=pl.BlockSpec((heads, rows, width // heads), lambda i: (0, 0, 0)),
        compiler_params=pltpu.CompilerParams(vmem_limit_bytes=SMALL_LIMIT * 1024 * 1024),
        cost_estimate=pl.CostEstimate(flops=2 * rows * width * width, bytes_accessed=4 * width * (rows + width), transcendentals=0),
        name="query",
    )(*(pltpu.with_memory_space_constraint(x, pltpu.HBM) for x in (tokens, weight)))


def pair_sum_kernel(keep_ref, got_ref, *out_refs):
    rows = out_refs[0].shape[0]
    for index, out_ref in enumerate(out_refs):
        slot, part = index // 2, slice(index % 2 * rows, (index % 2 + 1) * rows)
        out_ref[...] = (keep_ref[slot, part].astype(F32) + got_ref[slot, part].astype(F32)).astype(BF16)


def plane_sum_kernel(*refs):
    *parts, main_ref, up_ref = refs
    main = main_ref.shape[0]
    count = len(parts) // 2
    total = [sum(part[...].astype(F32) for part in parts[start : start + count]).astype(BF16) for start in (0, count)]
    total = jnp.concatenate(total, axis=0)
    main_ref[...] = total[:main]
    up_ref[...] = total[main:]


def sum_kernel(*refs):
    *parts, out_ref = refs
    total = parts[0][...].astype(F32)
    for part in parts[1:]:
        total = total + part[...].astype(F32)
    out_ref[...] = total.astype(BF16)


def stepped(totals, bases):
    norms = [jnp.sqrt(jnp.sum(total * total)) for total in totals]
    iterates = [(total / (norm + 1e-07)).astype(BF16) for total, norm in zip(totals, norms)]
    for step in range(NS_STEPS):
        grams = [mm(x, x, NT).astype(BF16) for x in iterates]
        squares = [mm(g, g, NN) for g in grams]
        mixers = [(coef_b * g.astype(F32) + coef_c * s).astype(BF16) for g, s in zip(grams, squares)]
        moved = [mm(m, x, NN) for m, x in zip(mixers, iterates)]
        iterates = [(coef_a * x.astype(F32) + y).astype(BF16) for x, y in zip(iterates, moved)]
    return [(base - step_size * x.astype(F32)).astype(BF16) for base, x in zip(bases, iterates)]


def newton_kernel(heads, mine_ref, other_ref, half_ref, got_ref, base_ref, base_up_ref, out_ref, *part_refs):
    head_dim, half = mine_ref.shape[0], half_ref.shape[0]
    even = position(heads)[1] == 0
    a, b = half_ref[...], got_ref[...]
    upper = jnp.concatenate([jnp.where(even, a, b), jnp.where(even, b, a)], axis=0).astype(F32)
    main, upper = stepped((mine_ref[...].astype(F32) + other_ref[...].astype(F32), upper), (base_ref[...], base_up_ref[...]))
    whole = jnp.concatenate([main, jnp.where(even, upper[:half], upper[half:])], axis=0)
    out_ref[...] = whole
    rows = whole.shape[0] // len(part_refs)
    for index, part_ref in enumerate(part_refs):
        part_ref[...] = whole[index * rows : (index + 1) * rows]


def head_output(even, q, here, there):
    head_dim = q.shape[1]
    here, there = (jnp.concatenate([ref[...] for ref in refs], axis=0) for refs in (here, there))
    a, b = jnp.where(even, here, there), jnp.where(even, there, here)
    up_b = jnp.concatenate([a[head_dim:], b[head_dim:]], axis=0)
    gate = mm(q, a[:head_dim], NN)
    upper = mm(q, up_b, NN)
    hidden = (gate * jax.nn.sigmoid(gate) * upper).astype(BF16)
    return mm(hidden, b[:head_dim], NT).astype(BF16)


def apply_kernel(far, q_ref, *refs):
    *block_refs, out_ref = refs
    half = len(block_refs) // 2
    own, core = position(q_ref.shape[0])
    out_ref[...] = head_output(core == 0, q_ref[own ^ far], block_refs[:half], block_refs[half:])


def finish_kernel(q_ref, *refs):
    *piece_refs, first_ref, second_ref, first_there_ref, second_there_ref, out_hbm, pieces, whole, sems = refs
    heads, rows, head_dim = q_ref.shape
    own, core = position(heads)
    lot = rows // FINISH_LOTS
    copies = []
    for index in range(FINISH_LOTS):
        part = pl.ds(index * lot, lot)
        for far, piece_ref in enumerate(piece_refs):
            pieces[far, part] = piece_ref[part]
        q = q_ref[own ^ (heads - 1), part]
        pieces[heads - 1, part] = head_output(core == 0, q, (first_ref, second_ref), (first_there_ref, second_there_ref))
        for head in range(heads):
            whole[part, head * head_dim : (head + 1) * head_dim] = pieces[own ^ head, part]
        copies.append(pltpu.make_async_copy(whole.at[part], out_hbm.at[part], sems.at[index]))
        copies[-1].start()
    for copy in copies:
        copy.wait()


def finish(query, pieces, blocks):
    heads, rows, head_dim = query.shape
    operands = [pltpu.with_memory_space_constraint(x, pltpu.VMEM) for x in (query, *pieces, *blocks)]
    return pl.pallas_call(
        finish_kernel,
        out_shape=jax.ShapeDtypeStruct((rows, heads * head_dim), BF16),
        in_specs=[pl.BlockSpec(memory_space=pltpu.VMEM)] * len(operands),
        out_specs=pl.BlockSpec(memory_space=pl.ANY),
        scratch_shapes=[
            pltpu.VMEM((heads, rows, head_dim), BF16),
            pltpu.VMEM((rows, heads * head_dim), BF16),
            pltpu.SemaphoreType.DMA((FINISH_LOTS,)),
        ],
        compiler_params=pltpu.CompilerParams(vmem_limit_bytes=SMALL_LIMIT * 1024 * 1024),
        name="finish",
    )(*operands)


def shards(tokens, qkv_weight, w_gate, w_up, w_down, view_kind):
    rows, width = tokens.shape
    heads, head_dim, hidden = w_gate.shape
    groups = lax.axis_size("tok")
    own, core = position(heads)
    w_down_t = jnp.transpose(w_down, (0, 2, 1))
    half = head_dim // 2
    shape = lambda *dims: pltpu.VMEM(dims, BF16)
    size = head_dim * hidden
    main_block, half_block = shape(head_dim, hidden), shape(half, hidden)
    size = head_dim * hidden

    def exchange(x, bits):
        return lax.ppermute(x, "tok", [(i, i ^ bits) for i in range(groups)])

    keep, give = gradients(view_kind, tokens, qkv_weight, w_gate, w_up, w_down_t)
    got = exchange(give, 1)
    block = shape(head_dim + half, hidden)
    part_block = shape(block.shape[0] // 2, hidden)
    sums = small(pair_sum_kernel, [part_block] * (2 * heads), (keep, got), 9 * keep.size, "pair_sum")
    first, second = sums[0::2], sums[1::2]
    first_on, second_on = exchange(first[3], 2), exchange(second[3], 4)
    first_in, second_in = exchange(first[1], 2), exchange(second[2], 4)
    first_on = exchange(small(sum_kernel, part_block, (first[2], first_on), 6 * size, "pass_sum"), 4)
    second_on = exchange(small(sum_kernel, part_block, (second[1], second_on), 6 * size, "pass_sum"), 2)
    parts = (first[0], first_in, first_on, second[0], second_in, second_on)
    main, upper = small(plane_sum_kernel, [main_block, half_block], parts, 10 * size, "plane_sum")
    query = project_query(tokens, qkv_weight, heads)
    base = jnp.where(core == 0, lax.dynamic_index_in_dim(w_gate, own, 0, False), lax.dynamic_index_in_dim(w_down_t, own, 0, False))
    base_up = lax.dynamic_index_in_dim(w_up, own, 0, False)

    def over_line(total, name):
        bits = 2 * heads
        while bits < groups // 2:
            total = small(sum_kernel, shape(*total.shape), (total, exchange(total, bits)), 6 * total.size, name)
            bits *= 2
        return total, exchange(total, bits)

    upper, upper_other = over_line(upper, "line_sum_up")
    upper_other, query, base, base_up = lax.optimization_barrier((upper_other, query, base, base_up))
    main, main_other = over_line(main, "line_sum")
    upper = small(sum_kernel, half_block, (upper, upper_other), 10 * size, "up_sum")
    upper_got = exchange(upper, 1)
    fresh, first, second = small(
        functools.partial(newton_kernel, heads), [block, part_block, part_block], (main, main_other, upper, upper_got, base, base_up), 30 * size, "newton"
    )

    def apply(far, *args):
        return small(functools.partial(apply_kernel, far), shape(rows, head_dim), (query, *args), 20 * rows * head_dim, "apply")

    over_y, over_z = [exchange(x, 2) for x in (first, second)], [exchange(x, 4) for x in (first, second)]
    across = [exchange(over_y[0], 4), exchange(over_z[1], 2)]
    swapped = lambda blocks: (*blocks, *(exchange(x, 1) for x in blocks))
    piece = apply(0, fresh, exchange(fresh, 1))
    over_y, over_z, piece = lax.optimization_barrier((over_y, over_z, piece))
    pieces = [piece, apply(1, *swapped(over_y)), apply(2, *swapped(over_z))]
    return finish(query, pieces, swapped(across))


def solution(mesh):
    placed = (P(("scene", "tok"), None), P(), P(), P(), P(), P("scene"))
    return jax.shard_map(
        shards, mesh=mesh, in_specs=placed, out_specs=P(("scene", "tok"), None), check_vma=False
    )
```

```python
import functools

import jax
import jax.numpy as jnp
from jax import lax
from jax.experimental import pallas as pl
from jax.experimental.pallas import tpu as pltpu
from jax.sharding import PartitionSpec as P

VIEWS = 16
NS_STEPS = 5
BF16 = jnp.bfloat16
F32 = jnp.float32
K1_LIMIT = 40
SMALL_LIMIT = 24
FINISH_LOTS = 2

coef_a = 3.4445
coef_b = -4.775
coef_c = 2.0315
step_size = 0.8


def mm(a, b, dims):
    return lax.dot_general(a, b, (dims, ((), ())), preferred_element_type=F32)


NN = ((1,), (0,))
NT = ((1,), (1,))
TN = ((0,), (0,))


def position(heads):
    place = lax.axis_index("tok")
    return lax.rem(lax.div(place, 2), heads), lax.rem(place, 2)


def grad_kernel(
    view_hbm, tok_hbm, qkv_hbm, gate_hbm, up_hbm, down_hbm, keep_ref, give_ref, view, tok, wkv, fast, kv, both_w, down_w, sems
):
    rows, width = tok.shape
    heads, head_dim = kv.shape[1], kv.shape[3]
    hidden = down_w.shape[2]
    half = head_dim // 2
    own, core = position(heads)
    owner = lax.div(lax.axis_index("tok") * rows, rows * lax.axis_size("tok") // VIEWS)
    count = iter(range(4 + 3 * heads))

    def fetch(source, target):
        copy = pltpu.make_async_copy(source, target, sems.at[next(count)])
        copy.start()
        return copy

    tok_copy = fetch(tok_hbm, tok)
    kv_copies = [fetch(qkv_hbm.at[:, (1 + which) * width : (2 + which) * width], wkv.at[which]) for which in range(2)]
    view_copy = fetch(view_hbm, view)
    fast_copies = [
        fetch(ref.at[head], fast.at[head, i]) for head in range(heads) for i, ref in enumerate((gate_hbm, up_hbm, down_hbm))
    ]
    tok_copy.wait()
    view_copy.wait()
    flag = view[owner].astype(F32)
    for which in range(2):
        kv_copies[which].wait()
        for pair in range(heads // 2):
            columns = slice(2 * pair * head_dim, (2 * pair + 2) * head_dim)
            part = mm(tok[...], wkv[which, :, columns], NN).astype(BF16)
            if which == 1:
                part = (part.astype(F32) * flag).astype(BF16)
            kv[which, 2 * pair] = part[:, :head_dim]
            kv[which, 2 * pair + 1] = part[:, head_dim:]
    for copy in fast_copies:
        copy.wait()
    for head in range(heads):
        both_w[head, :, :hidden] = fast[head, 0].astype(BF16)
        both_w[head, :, hidden:] = fast[head, 1].astype(BF16)
        down_w[head] = fast[head, 2].astype(BF16)
    even = core == 0
    chunk = rows // 2
    for head in range(heads):
        both_sum = down_sum = None
        for start in range(0, rows, chunk):
            k = kv[0, head, start : start + chunk, :]
            v = kv[1, head, start : start + chunk, :]
            both = mm(k, both_w[head], NN)
            dhid = -mm(v, down_w[head], NN)
            gate, upper = both[:, :hidden], both[:, hidden:]
            sig = jax.nn.sigmoid(gate)
            act = gate * sig
            hid = (act * upper).astype(BF16)
            dgate = (dhid * upper * (sig * (1.0 + gate * (1.0 - sig)))).astype(BF16)
            dup = (dhid * act).astype(BF16)
            both_part = mm(k, jnp.concatenate([dgate, dup], axis=1), TN)
            down_part = mm(v, hid, TN)
            both_sum = both_part if both_sum is None else both_sum + both_part
            down_sum = down_part if down_sum is None else down_sum + down_part
        gate_g = both_sum[:, :hidden].astype(BF16)
        up_g = both_sum[:, hidden:].astype(BF16)
        down_g = (-down_sum).astype(BF16)
        slot = own ^ head
        keep_ref[slot, half:] = jnp.where(even, gate_g, down_g)
        give_ref[slot, half:] = jnp.where(even, down_g, gate_g)
        keep_ref[slot, :half] = jnp.where(even, up_g[:half], up_g[half:])
        give_ref[slot, :half] = jnp.where(even, up_g[half:], up_g[:half])


def gradients(view_kind, tokens, qkv_weight, w_gate, w_up, w_down_t):
    rows, width = tokens.shape
    heads, head_dim, hidden = w_gate.shape
    args = [pltpu.with_memory_space_constraint(x, pltpu.HBM) for x in (view_kind, tokens, qkv_weight, w_gate, w_up, w_down_t)]
    shape = pltpu.VMEM((heads, head_dim * 3 // 2, hidden), BF16)
    return pl.pallas_call(
        grad_kernel,
        out_shape=[shape] * 2,
        in_specs=[pl.BlockSpec(memory_space=pl.ANY)] * 6,
        out_specs=[pl.BlockSpec(memory_space=pltpu.VMEM)] * 2,
        scratch_shapes=[
            pltpu.SMEM(view_kind.shape, jnp.int32),
            pltpu.VMEM((rows, width), BF16),
            pltpu.VMEM((2, width, width), BF16),
            pltpu.VMEM((heads, 3, head_dim, hidden), F32),
            pltpu.VMEM((2, heads, rows, head_dim), BF16),
            pltpu.VMEM((heads, head_dim, 2 * hidden), BF16),
            pltpu.VMEM((heads, head_dim, hidden), BF16),
            pltpu.SemaphoreType.DMA((4 + 3 * heads,)),
        ],
        compiler_params=pltpu.CompilerParams(vmem_limit_bytes=K1_LIMIT * 1024 * 1024),
        cost_estimate=pl.CostEstimate(
            flops=4 * rows * width * width + 12 * heads * rows * head_dim * hidden,
            bytes_accessed=2 * rows * width + 4 * width * width + 12 * heads * head_dim * hidden,
            transcendentals=heads * rows * hidden,
        ),
        name="gradients",
    )(*args)


def small(kernel, shapes, operands, nbytes, name):
    specs = [pl.BlockSpec(memory_space=pltpu.VMEM)] * len(operands)
    operands = [pltpu.with_memory_space_constraint(x, pltpu.VMEM) for x in operands]
    return pl.pallas_call(
        kernel,
        out_shape=shapes,
        in_specs=specs,
        compiler_params=pltpu.CompilerParams(vmem_limit_bytes=SMALL_LIMIT * 1024 * 1024),
        cost_estimate=pl.CostEstimate(flops=0, bytes_accessed=nbytes, transcendentals=0),
        name=name,
    )(*operands)


def query_kernel(tokens_ref, weight_ref, out_ref):
    heads, _, head_dim = out_ref.shape
    part = mm(tokens_ref[...], weight_ref[...], NN).astype(BF16)
    for head in range(heads):
        out_ref[head] = part[:, head * head_dim : (head + 1) * head_dim]


def project_query(tokens, weight, heads):
    rows, width = tokens.shape
    return pl.pallas_call(
        query_kernel,
        out_shape=pltpu.VMEM((heads, rows, width // heads), BF16),
        grid=(1,),
        in_specs=[pl.BlockSpec((rows, width), lambda i: (0, 0)), pl.BlockSpec((width, width), lambda i: (0, 0))],
        out_specs=pl.BlockSpec((heads, rows, width // heads), lambda i: (0, 0, 0)),
        compiler_params=pltpu.CompilerParams(vmem_limit_bytes=SMALL_LIMIT * 1024 * 1024),
        cost_estimate=pl.CostEstimate(flops=2 * rows * width * width, bytes_accessed=4 * width * (rows + width), transcendentals=0),
        name="query",
    )(*(pltpu.with_memory_space_constraint(x, pltpu.HBM) for x in (tokens, weight)))


def pair_sum_kernel(keep_ref, got_ref, *out_refs):
    rows = out_refs[0].shape[0]
    for index, out_ref in enumerate(out_refs):
        slot, part = index // 2, slice(index % 2 * rows, (index % 2 + 1) * rows)
        out_ref[...] = (keep_ref[slot, part].astype(F32) + got_ref[slot, part].astype(F32)).astype(BF16)


def up_sum_kernel(mine_ref, other_ref, out_ref):
    half = out_ref.shape[0]
    out_ref[...] = (mine_ref[:half].astype(F32) + other_ref[:half].astype(F32)).astype(BF16)


def sum_kernel(*refs):
    *parts, out_ref = refs
    total = parts[0][...].astype(F32)
    for part in parts[1:]:
        total = total + part[...].astype(F32)
    out_ref[...] = total.astype(BF16)


def stepped(totals, bases):
    norms = [jnp.sqrt(jnp.sum(total * total)) for total in totals]
    iterates = [(total / (norm + 1e-07)).astype(BF16) for total, norm in zip(totals, norms)]
    for step in range(NS_STEPS):
        grams = [mm(x, x, NT).astype(BF16) for x in iterates]
        squares = [mm(g, g, NN) for g in grams]
        mixers = [(coef_b * g.astype(F32) + coef_c * s).astype(BF16) for g, s in zip(grams, squares)]
        moved = [mm(m, x, NN) for m, x in zip(mixers, iterates)]
        iterates = [(coef_a * x.astype(F32) + y).astype(BF16) for x, y in zip(iterates, moved)]
    return [(base - step_size * x.astype(F32)).astype(BF16) for base, x in zip(bases, iterates)]


def newton_kernel(
    heads, first_ref, first_other_ref, second_ref, second_other_ref, half_ref, got_ref, base_ref, base_up_ref, out_ref, *part_refs
):
    half = half_ref.shape[0]
    even = position(heads)[1] == 0
    a, b = half_ref[...], got_ref[...]
    upper = jnp.concatenate([jnp.where(even, a, b), jnp.where(even, b, a)], axis=0).astype(F32)
    first = first_ref[half:].astype(F32) + first_other_ref[half:].astype(F32)
    second = second_ref[...].astype(F32) + second_other_ref[...].astype(F32)
    main, upper = stepped((jnp.concatenate([first, second], axis=0), upper), (base_ref[...], base_up_ref[...]))
    whole = jnp.concatenate([jnp.where(even, upper[:half], upper[half:]), main], axis=0)
    out_ref[...] = whole
    rows = whole.shape[0] // len(part_refs)
    for index, part_ref in enumerate(part_refs):
        part_ref[...] = whole[index * rows : (index + 1) * rows]


def head_output(even, q, here, there):
    head_dim = q.shape[1]
    here, there = (jnp.concatenate([ref[...] for ref in refs], axis=0) for refs in (here, there))
    a, b = jnp.where(even, here, there), jnp.where(even, there, here)
    half = head_dim // 2
    up_b = jnp.concatenate([a[:half], b[:half]], axis=0)
    gate = mm(q, a[half:], NN)
    upper = mm(q, up_b, NN)
    hidden = (gate * jax.nn.sigmoid(gate) * upper).astype(BF16)
    return mm(hidden, b[half:], NT).astype(BF16)


def apply_kernel(far, q_ref, *refs):
    *block_refs, out_ref = refs
    half = len(block_refs) // 2
    own, core = position(q_ref.shape[0])
    out_ref[...] = head_output(core == 0, q_ref[own ^ far], block_refs[:half], block_refs[half:])


def finish_kernel(q_ref, *refs):
    *piece_refs, first_ref, second_ref, first_there_ref, second_there_ref, out_hbm, pieces, whole, sems = refs
    heads, rows, head_dim = q_ref.shape
    own, core = position(heads)
    lot = rows // FINISH_LOTS
    copies = []
    for index in range(FINISH_LOTS):
        part = pl.ds(index * lot, lot)
        for far, piece_ref in enumerate(piece_refs):
            pieces[far, part] = piece_ref[part]
        q = q_ref[own ^ (heads - 1), part]
        pieces[heads - 1, part] = head_output(core == 0, q, (first_ref, second_ref), (first_there_ref, second_there_ref))
        for head in range(heads):
            whole[part, head * head_dim : (head + 1) * head_dim] = pieces[own ^ head, part]
        copies.append(pltpu.make_async_copy(whole.at[part], out_hbm.at[part], sems.at[index]))
        copies[-1].start()
    for copy in copies:
        copy.wait()


def finish(query, pieces, blocks):
    heads, rows, head_dim = query.shape
    operands = [pltpu.with_memory_space_constraint(x, pltpu.VMEM) for x in (query, *pieces, *blocks)]
    return pl.pallas_call(
        finish_kernel,
        out_shape=jax.ShapeDtypeStruct((rows, heads * head_dim), BF16),
        in_specs=[pl.BlockSpec(memory_space=pltpu.VMEM)] * len(operands),
        out_specs=pl.BlockSpec(memory_space=pl.ANY),
        scratch_shapes=[
            pltpu.VMEM((heads, rows, head_dim), BF16),
            pltpu.VMEM((rows, heads * head_dim), BF16),
            pltpu.SemaphoreType.DMA((FINISH_LOTS,)),
        ],
        compiler_params=pltpu.CompilerParams(vmem_limit_bytes=SMALL_LIMIT * 1024 * 1024),
        name="finish",
    )(*operands)


def shards(tokens, qkv_weight, w_gate, w_up, w_down, view_kind):
    rows, width = tokens.shape
    heads, head_dim, hidden = w_gate.shape
    groups = lax.axis_size("tok")
    own, core = position(heads)
    w_down_t = jnp.transpose(w_down, (0, 2, 1))
    half = head_dim // 2
    shape = lambda *dims: pltpu.VMEM(dims, BF16)
    size = head_dim * hidden
    main_block, half_block = shape(head_dim, hidden), shape(half, hidden)
    size = head_dim * hidden

    def exchange(x, bits):
        return lax.ppermute(x, "tok", [(i, i ^ bits) for i in range(groups)])

    keep, give = gradients(view_kind, tokens, qkv_weight, w_gate, w_up, w_down_t)
    got = exchange(give, 1)
    block = shape(head_dim + half, hidden)
    part_block = shape(block.shape[0] // 2, hidden)
    sums = small(pair_sum_kernel, [part_block] * (2 * heads), (keep, got), 9 * keep.size, "pair_sum")
    first, second = sums[0::2], sums[1::2]
    first_on, second_on = exchange(first[3], 2), exchange(second[3], 4)
    first_in, second_in = exchange(first[1], 2), exchange(second[2], 4)
    first_on = exchange(small(sum_kernel, part_block, (first[2], first_on), 6 * size, "pass_sum"), 4)
    second_on = exchange(small(sum_kernel, part_block, (second[1], second_on), 6 * size, "pass_sum"), 2)
    first = small(sum_kernel, part_block, (first[0], first_in, first_on), 8 * size, "plane_sum")
    second = small(sum_kernel, part_block, (second[0], second_in, second_on), 8 * size, "plane_sum")
    query = project_query(tokens, qkv_weight, heads)
    base = jnp.where(core == 0, lax.dynamic_index_in_dim(w_gate, own, 0, False), lax.dynamic_index_in_dim(w_down_t, own, 0, False))
    base_up = lax.dynamic_index_in_dim(w_up, own, 0, False)

    def over_line(total, name):
        bits = 2 * heads
        while bits < groups // 2:
            total = small(sum_kernel, shape(*total.shape), (total, exchange(total, bits)), 6 * total.size, name)
            bits *= 2
        return total, exchange(total, bits)

    first, first_other = over_line(first, "line_sum")
    second, second_other = over_line(second, "line_sum")
    first_other, query, base, base_up = lax.optimization_barrier((first_other, query, base, base_up))
    upper = small(up_sum_kernel, half_block, (first, first_other), 6 * size, "up_sum")
    args = (first, first_other, second, second_other, upper, exchange(upper, 1), base, base_up)
    kernel = functools.partial(newton_kernel, heads)
    fresh, first, second = small(kernel, [block, part_block, part_block], args, 30 * size, "newton")

    def apply(far, *args):
        return small(functools.partial(apply_kernel, far), shape(rows, head_dim), (query, *args), 20 * rows * head_dim, "apply")

    over_y, over_z = [exchange(x, 2) for x in (first, second)], [exchange(x, 4) for x in (first, second)]
    across = [exchange(over_y[0], 4), exchange(over_z[1], 2)]
    swapped = lambda blocks: (*blocks, *(exchange(x, 1) for x in blocks))
    piece = apply(0, fresh, exchange(fresh, 1))
    over_y, over_z, piece = lax.optimization_barrier((over_y, over_z, piece))
    pieces = [piece, apply(1, *swapped(over_y)), apply(2, *swapped(over_z))]
    return finish(query, pieces, swapped(across))


def solution(mesh):
    placed = (P(("scene", "tok"), None), P(), P(), P(), P(), P("scene"))
    return jax.shard_map(
        shards, mesh=mesh, in_specs=placed, out_specs=P(("scene", "tok"), None), check_vma=False
    )
```

```python
import functools

import jax
import jax.numpy as jnp
from jax import lax
from jax.experimental import pallas as pl
from jax.experimental.pallas import tpu as pltpu
from jax.sharding import PartitionSpec as P

VIEWS = 16
NS_STEPS = 5
BF16 = jnp.bfloat16
F32 = jnp.float32
K1_LIMIT = 40
SMALL_LIMIT = 24
FINISH_LOTS = 2

coef_a = 3.4445
coef_b = -4.775
coef_c = 2.0315
step_size = 0.8


def mm(a, b, dims):
    return lax.dot_general(a, b, (dims, ((), ())), preferred_element_type=F32)


NN = ((1,), (0,))
NT = ((1,), (1,))
TN = ((0,), (0,))


def position(heads):
    place = lax.axis_index("tok")
    return lax.rem(lax.div(place, 2), heads), lax.rem(place, 2)


def grad_kernel(
    view_hbm, tok_hbm, qkv_hbm, gate_hbm, up_hbm, down_hbm, first_keep_ref, second_keep_ref, first_give_ref, second_give_ref, view, tok, wkv, fast, kv, both_w, down_w, sems
):
    rows, width = tok.shape
    heads, head_dim = kv.shape[1], kv.shape[3]
    hidden = down_w.shape[2]
    half = head_dim // 2
    own, core = position(heads)
    owner = lax.div(lax.axis_index("tok") * rows, rows * lax.axis_size("tok") // VIEWS)
    count = iter(range(4 + 3 * heads))

    def fetch(source, target):
        copy = pltpu.make_async_copy(source, target, sems.at[next(count)])
        copy.start()
        return copy

    tok_copy = fetch(tok_hbm, tok)
    kv_copies = [fetch(qkv_hbm.at[:, (1 + which) * width : (2 + which) * width], wkv.at[which]) for which in range(2)]
    view_copy = fetch(view_hbm, view)
    fast_copies = [
        fetch(ref.at[head], fast.at[head, i]) for head in range(heads) for i, ref in enumerate((gate_hbm, up_hbm, down_hbm))
    ]
    tok_copy.wait()
    view_copy.wait()
    flag = view[owner].astype(F32)
    for which in range(2):
        kv_copies[which].wait()
        for pair in range(heads // 2):
            columns = slice(2 * pair * head_dim, (2 * pair + 2) * head_dim)
            part = mm(tok[...], wkv[which, :, columns], NN).astype(BF16)
            if which == 1:
                part = (part.astype(F32) * flag).astype(BF16)
            kv[which, 2 * pair] = part[:, :head_dim]
            kv[which, 2 * pair + 1] = part[:, head_dim:]
    for copy in fast_copies:
        copy.wait()
    for head in range(heads):
        both_w[head, :, :hidden] = fast[head, 0].astype(BF16)
        both_w[head, :, hidden:] = fast[head, 1].astype(BF16)
        down_w[head] = fast[head, 2].astype(BF16)
    even = core == 0
    chunk = rows // 2
    for head in range(heads):
        both_sum = down_sum = None
        for start in range(0, rows, chunk):
            k = kv[0, head, start : start + chunk, :]
            v = kv[1, head, start : start + chunk, :]
            both = mm(k, both_w[head], NN)
            dhid = -mm(v, down_w[head], NN)
            gate, upper = both[:, :hidden], both[:, hidden:]
            sig = jax.nn.sigmoid(gate)
            act = gate * sig
            hid = (act * upper).astype(BF16)
            dgate = (dhid * upper * (sig * (1.0 + gate * (1.0 - sig)))).astype(BF16)
            dup = (dhid * act).astype(BF16)
            both_part = mm(k, jnp.concatenate([dgate, dup], axis=1), TN)
            down_part = mm(v, hid, TN)
            both_sum = both_part if both_sum is None else both_sum + both_part
            down_sum = down_part if down_sum is None else down_sum + down_part
        gate_g = both_sum[:, :hidden].astype(BF16)
        up_g = both_sum[:, hidden:].astype(BF16)
        down_g = (-down_sum).astype(BF16)
        slot = own ^ head
        keep = jnp.concatenate([jnp.where(even, up_g[:half], up_g[half:]), jnp.where(even, gate_g, down_g)], axis=0)
        give = jnp.concatenate([jnp.where(even, up_g[half:], up_g[:half]), jnp.where(even, down_g, gate_g)], axis=0)
        cut = keep.shape[0] // 2
        first_keep_ref[slot], second_keep_ref[slot] = keep[:cut], keep[cut:]
        first_give_ref[slot], second_give_ref[slot] = give[:cut], give[cut:]


def gradients(view_kind, tokens, qkv_weight, w_gate, w_up, w_down_t):
    rows, width = tokens.shape
    heads, head_dim, hidden = w_gate.shape
    args = [pltpu.with_memory_space_constraint(x, pltpu.HBM) for x in (view_kind, tokens, qkv_weight, w_gate, w_up, w_down_t)]
    shape = pltpu.VMEM((heads, head_dim * 3 // 4, hidden), BF16)
    return pl.pallas_call(
        grad_kernel,
        out_shape=[shape] * 4,
        in_specs=[pl.BlockSpec(memory_space=pl.ANY)] * 6,
        out_specs=[pl.BlockSpec(memory_space=pltpu.VMEM)] * 4,
        scratch_shapes=[
            pltpu.SMEM(view_kind.shape, jnp.int32),
            pltpu.VMEM((rows, width), BF16),
            pltpu.VMEM((2, width, width), BF16),
            pltpu.VMEM((heads, 3, head_dim, hidden), F32),
            pltpu.VMEM((2, heads, rows, head_dim), BF16),
            pltpu.VMEM((heads, head_dim, 2 * hidden), BF16),
            pltpu.VMEM((heads, head_dim, hidden), BF16),
            pltpu.SemaphoreType.DMA((4 + 3 * heads,)),
        ],
        compiler_params=pltpu.CompilerParams(vmem_limit_bytes=K1_LIMIT * 1024 * 1024),
        cost_estimate=pl.CostEstimate(
            flops=4 * rows * width * width + 12 * heads * rows * head_dim * hidden,
            bytes_accessed=2 * rows * width + 4 * width * width + 12 * heads * head_dim * hidden,
            transcendentals=heads * rows * hidden,
        ),
        name="gradients",
    )(*args)


def small(kernel, shapes, operands, nbytes, name):
    specs = [pl.BlockSpec(memory_space=pltpu.VMEM)] * len(operands)
    operands = [pltpu.with_memory_space_constraint(x, pltpu.VMEM) for x in operands]
    return pl.pallas_call(
        kernel,
        out_shape=shapes,
        in_specs=specs,
        compiler_params=pltpu.CompilerParams(vmem_limit_bytes=SMALL_LIMIT * 1024 * 1024),
        cost_estimate=pl.CostEstimate(flops=0, bytes_accessed=nbytes, transcendentals=0),
        name=name,
    )(*operands)


def query_kernel(tokens_ref, weight_ref, out_ref):
    heads, _, head_dim = out_ref.shape
    part = mm(tokens_ref[...], weight_ref[...], NN).astype(BF16)
    for head in range(heads):
        out_ref[head] = part[:, head * head_dim : (head + 1) * head_dim]


def project_query(tokens, weight, heads):
    rows, width = tokens.shape
    return pl.pallas_call(
        query_kernel,
        out_shape=pltpu.VMEM((heads, rows, width // heads), BF16),
        grid=(1,),
        in_specs=[pl.BlockSpec((rows, width), lambda i: (0, 0)), pl.BlockSpec((width, width), lambda i: (0, 0))],
        out_specs=pl.BlockSpec((heads, rows, width // heads), lambda i: (0, 0, 0)),
        compiler_params=pltpu.CompilerParams(vmem_limit_bytes=SMALL_LIMIT * 1024 * 1024),
        cost_estimate=pl.CostEstimate(flops=2 * rows * width * width, bytes_accessed=4 * width * (rows + width), transcendentals=0),
        name="query",
    )(*(pltpu.with_memory_space_constraint(x, pltpu.HBM) for x in (tokens, weight)))


def pair_sum_kernel(keep_ref, got_ref, *out_refs):
    for slot, out_ref in enumerate(out_refs):
        out_ref[...] = (keep_ref[slot].astype(F32) + got_ref[slot].astype(F32)).astype(BF16)


def up_sum_kernel(mine_ref, other_ref, out_ref):
    half = out_ref.shape[0]
    out_ref[...] = (mine_ref[:half].astype(F32) + other_ref[:half].astype(F32)).astype(BF16)


def sum_kernel(*refs):
    *parts, out_ref = refs
    total = parts[0][...].astype(F32)
    for part in parts[1:]:
        total = total + part[...].astype(F32)
    out_ref[...] = total.astype(BF16)


def stepped(totals, bases):
    norms = [jnp.sqrt(jnp.sum(total * total)) for total in totals]
    iterates = [(total / (norm + 1e-07)).astype(BF16) for total, norm in zip(totals, norms)]
    for step in range(NS_STEPS):
        grams = [mm(x, x, NT).astype(BF16) for x in iterates]
        squares = [mm(g, g, NN) for g in grams]
        mixers = [(coef_b * g.astype(F32) + coef_c * s).astype(BF16) for g, s in zip(grams, squares)]
        moved = [mm(m, x, NN) for m, x in zip(mixers, iterates)]
        iterates = [(coef_a * x.astype(F32) + y).astype(BF16) for x, y in zip(iterates, moved)]
    return [(base - step_size * x.astype(F32)).astype(BF16) for base, x in zip(bases, iterates)]


def newton_kernel(
    heads, first_ref, first_other_ref, second_ref, second_other_ref, half_ref, got_ref, base_ref, base_up_ref, out_ref, *part_refs
):
    half = half_ref.shape[0]
    even = position(heads)[1] == 0
    a, b = half_ref[...], got_ref[...]
    upper = jnp.concatenate([jnp.where(even, a, b), jnp.where(even, b, a)], axis=0).astype(F32)
    first = first_ref[half:].astype(F32) + first_other_ref[half:].astype(F32)
    second = second_ref[...].astype(F32) + second_other_ref[...].astype(F32)
    main, upper = stepped((jnp.concatenate([first, second], axis=0), upper), (base_ref[...], base_up_ref[...]))
    whole = jnp.concatenate([jnp.where(even, upper[:half], upper[half:]), main], axis=0)
    out_ref[...] = whole
    rows = whole.shape[0] // len(part_refs)
    for index, part_ref in enumerate(part_refs):
        part_ref[...] = whole[index * rows : (index + 1) * rows]


def head_output(even, q, here, there):
    head_dim = q.shape[1]
    here, there = (jnp.concatenate([ref[...] for ref in refs], axis=0) for refs in (here, there))
    a, b = jnp.where(even, here, there), jnp.where(even, there, here)
    half = head_dim // 2
    up_b = jnp.concatenate([a[:half], b[:half]], axis=0)
    gate = mm(q, a[half:], NN)
    upper = mm(q, up_b, NN)
    hidden = (gate * jax.nn.sigmoid(gate) * upper).astype(BF16)
    return mm(hidden, b[half:], NT).astype(BF16)


def apply_kernel(far, q_ref, *refs):
    *block_refs, out_ref = refs
    half = len(block_refs) // 2
    own, core = position(q_ref.shape[0])
    out_ref[...] = head_output(core == 0, q_ref[own ^ far], block_refs[:half], block_refs[half:])


def finish_kernel(q_ref, *refs):
    *piece_refs, first_ref, second_ref, first_there_ref, second_there_ref, out_hbm, pieces, whole, sems = refs
    heads, rows, head_dim = q_ref.shape
    own, core = position(heads)
    lot = rows // FINISH_LOTS
    copies = []
    for index in range(FINISH_LOTS):
        part = pl.ds(index * lot, lot)
        for far, piece_ref in enumerate(piece_refs):
            pieces[far, part] = piece_ref[part]
        q = q_ref[own ^ (heads - 1), part]
        pieces[heads - 1, part] = head_output(core == 0, q, (first_ref, second_ref), (first_there_ref, second_there_ref))
        for head in range(heads):
            whole[part, head * head_dim : (head + 1) * head_dim] = pieces[own ^ head, part]
        copies.append(pltpu.make_async_copy(whole.at[part], out_hbm.at[part], sems.at[index]))
        copies[-1].start()
    for copy in copies:
        copy.wait()


def finish(query, pieces, blocks):
    heads, rows, head_dim = query.shape
    operands = [pltpu.with_memory_space_constraint(x, pltpu.VMEM) for x in (query, *pieces, *blocks)]
    return pl.pallas_call(
        finish_kernel,
        out_shape=jax.ShapeDtypeStruct((rows, heads * head_dim), BF16),
        in_specs=[pl.BlockSpec(memory_space=pltpu.VMEM)] * len(operands),
        out_specs=pl.BlockSpec(memory_space=pl.ANY),
        scratch_shapes=[
            pltpu.VMEM((heads, rows, head_dim), BF16),
            pltpu.VMEM((rows, heads * head_dim), BF16),
            pltpu.SemaphoreType.DMA((FINISH_LOTS,)),
        ],
        compiler_params=pltpu.CompilerParams(vmem_limit_bytes=SMALL_LIMIT * 1024 * 1024),
        name="finish",
    )(*operands)


def shards(tokens, qkv_weight, w_gate, w_up, w_down, view_kind):
    rows, width = tokens.shape
    heads, head_dim, hidden = w_gate.shape
    groups = lax.axis_size("tok")
    own, core = position(heads)
    w_down_t = jnp.transpose(w_down, (0, 2, 1))
    half = head_dim // 2
    shape = lambda *dims: pltpu.VMEM(dims, BF16)
    size = head_dim * hidden
    main_block, half_block = shape(head_dim, hidden), shape(half, hidden)
    size = head_dim * hidden

    def exchange(x, bits):
        return lax.ppermute(x, "tok", [(i, i ^ bits) for i in range(groups)])

    first, second, first_give, second_give = gradients(view_kind, tokens, qkv_weight, w_gate, w_up, w_down_t)
    block, part_block = shape(head_dim + half, hidden), shape((head_dim + half) // 2, hidden)
    first, second = (
        small(pair_sum_kernel, [part_block] * heads, (keep, exchange(give, 1)), 9 * keep.size, "pair_sum")
        for keep, give in ((first, first_give), (second, second_give))
    )
    first_on, second_on = exchange(first[3], 2), exchange(second[3], 4)
    first_in, second_in = exchange(first[1], 2), exchange(second[2], 4)
    first_on = exchange(small(sum_kernel, part_block, (first[2], first_on), 6 * size, "pass_sum"), 4)
    second_on = exchange(small(sum_kernel, part_block, (second[1], second_on), 6 * size, "pass_sum"), 2)
    first = small(sum_kernel, part_block, (first[0], first_in, first_on), 8 * size, "plane_sum")
    second = small(sum_kernel, part_block, (second[0], second_in, second_on), 8 * size, "plane_sum")
    query = project_query(tokens, qkv_weight, heads)
    base = jnp.where(core == 0, lax.dynamic_index_in_dim(w_gate, own, 0, False), lax.dynamic_index_in_dim(w_down_t, own, 0, False))
    base_up = lax.dynamic_index_in_dim(w_up, own, 0, False)

    def over_line(total, name):
        bits = 2 * heads
        while bits < groups // 2:
            total = small(sum_kernel, shape(*total.shape), (total, exchange(total, bits)), 6 * total.size, name)
            bits *= 2
        return total, exchange(total, bits)

    first, first_other = over_line(first, "line_sum")
    second, second_other = over_line(second, "line_sum")
    first_other, query, base, base_up = lax.optimization_barrier((first_other, query, base, base_up))
    upper = small(up_sum_kernel, half_block, (first, first_other), 6 * size, "up_sum")
    args = (first, first_other, second, second_other, upper, exchange(upper, 1), base, base_up)
    kernel = functools.partial(newton_kernel, heads)
    fresh, first, second = small(kernel, [block, part_block, part_block], args, 30 * size, "newton")

    def apply(far, *args):
        return small(functools.partial(apply_kernel, far), shape(rows, head_dim), (query, *args), 20 * rows * head_dim, "apply")

    over_y, over_z = [exchange(x, 2) for x in (first, second)], [exchange(x, 4) for x in (first, second)]
    across = [exchange(over_y[0], 4), exchange(over_z[1], 2)]
    swapped = lambda blocks: (*blocks, *(exchange(x, 1) for x in blocks))
    piece = apply(0, fresh, exchange(fresh, 1))
    over_y, over_z, piece = lax.optimization_barrier((over_y, over_z, piece))
    pieces = [piece, apply(1, *swapped(over_y)), apply(2, *swapped(over_z))]
    return finish(query, pieces, swapped(across))


def solution(mesh):
    placed = (P(("scene", "tok"), None), P(), P(), P(), P(), P("scene"))
    return jax.shard_map(
        shards, mesh=mesh, in_specs=placed, out_specs=P(("scene", "tok"), None), check_vma=False
    )
```

```python
import functools

import jax
import jax.numpy as jnp
from jax import lax
from jax.experimental import pallas as pl
from jax.experimental.pallas import tpu as pltpu
from jax.sharding import PartitionSpec as P

VIEWS = 16
NS_STEPS = 5
BF16 = jnp.bfloat16
F32 = jnp.float32
K1_LIMIT = 40
SMALL_LIMIT = 24
FINISH_LOTS = 2

coef_a = 3.4445
coef_b = -4.775
coef_c = 2.0315
step_size = 0.8


def mm(a, b, dims):
    return lax.dot_general(a, b, (dims, ((), ())), preferred_element_type=F32)


NN = ((1,), (0,))
NT = ((1,), (1,))
TN = ((0,), (0,))


def position(heads):
    place = lax.axis_index("tok")
    return lax.rem(lax.div(place, 2), heads), lax.rem(place, 2)


def grad_kernel(
    view_hbm, tok_hbm, qkv_hbm, gate_hbm, up_hbm, down_hbm, first_keep_ref, second_keep_ref, first_give_ref, second_give_ref, view, tok, wkv, fast, kv, both_w, down_w, sems
):
    rows, width = tok.shape
    heads, head_dim = kv.shape[1], kv.shape[3]
    hidden = down_w.shape[2]
    half = head_dim // 2
    own, core = position(heads)
    owner = lax.div(lax.axis_index("tok") * rows, rows * lax.axis_size("tok") // VIEWS)
    count = iter(range(4 + 3 * heads))

    def fetch(source, target):
        copy = pltpu.make_async_copy(source, target, sems.at[next(count)])
        copy.start()
        return copy

    tok_copy = fetch(tok_hbm, tok)
    kv_copies = [fetch(qkv_hbm.at[:, (1 + which) * width : (2 + which) * width], wkv.at[which]) for which in range(2)]
    view_copy = fetch(view_hbm, view)
    fast_copies = [
        fetch(ref.at[head], fast.at[head, i]) for head in range(heads) for i, ref in enumerate((gate_hbm, up_hbm, down_hbm))
    ]
    tok_copy.wait()
    view_copy.wait()
    flag = view[owner].astype(F32)
    for which in range(2):
        kv_copies[which].wait()
        for pair in range(heads // 2):
            columns = slice(2 * pair * head_dim, (2 * pair + 2) * head_dim)
            part = mm(tok[...], wkv[which, :, columns], NN).astype(BF16)
            if which == 1:
                part = (part.astype(F32) * flag).astype(BF16)
            kv[which, 2 * pair] = part[:, :head_dim]
            kv[which, 2 * pair + 1] = part[:, head_dim:]
    for copy in fast_copies:
        copy.wait()
    for head in range(heads):
        both_w[head, :, :hidden] = fast[head, 0].astype(BF16)
        both_w[head, :, hidden:] = fast[head, 1].astype(BF16)
        down_w[head] = fast[head, 2].astype(BF16)
    even = core == 0
    chunk = rows
    for head in range(heads):
        both_sum = down_sum = None
        for start in range(0, rows, chunk):
            k = kv[0, head, start : start + chunk, :]
            v = kv[1, head, start : start + chunk, :]
            both = mm(k, both_w[head], NN)
            dhid = -mm(v, down_w[head], NN)
            gate, upper = both[:, :hidden], both[:, hidden:]
            sig = jax.nn.sigmoid(gate)
            act = gate * sig
            hid = (act * upper).astype(BF16)
            dgate = (dhid * upper * (sig * (1.0 + gate * (1.0 - sig)))).astype(BF16)
            dup = (dhid * act).astype(BF16)
            both_part = mm(k, jnp.concatenate([dgate, dup], axis=1), TN)
            down_part = mm(v, hid, TN)
            both_sum = both_part if both_sum is None else both_sum + both_part
            down_sum = down_part if down_sum is None else down_sum + down_part
        gate_g = both_sum[:, :hidden].astype(BF16)
        up_g = both_sum[:, hidden:].astype(BF16)
        down_g = (-down_sum).astype(BF16)
        slot = own ^ head
        keep = jnp.concatenate([jnp.where(even, up_g[:half], up_g[half:]), jnp.where(even, gate_g, down_g)], axis=0)
        give = jnp.concatenate([jnp.where(even, up_g[half:], up_g[:half]), jnp.where(even, down_g, gate_g)], axis=0)
        cut = keep.shape[0] // 2
        first_keep_ref[slot], second_keep_ref[slot] = keep[:cut], keep[cut:]
        first_give_ref[slot], second_give_ref[slot] = give[:cut], give[cut:]


def gradients(view_kind, tokens, qkv_weight, w_gate, w_up, w_down_t):
    rows, width = tokens.shape
    heads, head_dim, hidden = w_gate.shape
    args = [pltpu.with_memory_space_constraint(x, pltpu.HBM) for x in (view_kind, tokens, qkv_weight, w_gate, w_up, w_down_t)]
    shape = pltpu.VMEM((heads, head_dim * 3 // 4, hidden), BF16)
    return pl.pallas_call(
        grad_kernel,
        out_shape=[shape] * 4,
        in_specs=[pl.BlockSpec(memory_space=pl.ANY)] * 6,
        out_specs=[pl.BlockSpec(memory_space=pltpu.VMEM)] * 4,
        scratch_shapes=[
            pltpu.SMEM(view_kind.shape, jnp.int32),
            pltpu.VMEM((rows, width), BF16),
            pltpu.VMEM((2, width, width), BF16),
            pltpu.VMEM((heads, 3, head_dim, hidden), F32),
            pltpu.VMEM((2, heads, rows, head_dim), BF16),
            pltpu.VMEM((heads, head_dim, 2 * hidden), BF16),
            pltpu.VMEM((heads, head_dim, hidden), BF16),
            pltpu.SemaphoreType.DMA((4 + 3 * heads,)),
        ],
        compiler_params=pltpu.CompilerParams(vmem_limit_bytes=K1_LIMIT * 1024 * 1024),
        cost_estimate=pl.CostEstimate(
            flops=4 * rows * width * width + 12 * heads * rows * head_dim * hidden,
            bytes_accessed=2 * rows * width + 4 * width * width + 12 * heads * head_dim * hidden,
            transcendentals=heads * rows * hidden,
        ),
        name="gradients",
    )(*args)


def small(kernel, shapes, operands, nbytes, name):
    specs = [pl.BlockSpec(memory_space=pltpu.VMEM)] * len(operands)
    operands = [pltpu.with_memory_space_constraint(x, pltpu.VMEM) for x in operands]
    return pl.pallas_call(
        kernel,
        out_shape=shapes,
        in_specs=specs,
        compiler_params=pltpu.CompilerParams(vmem_limit_bytes=SMALL_LIMIT * 1024 * 1024),
        cost_estimate=pl.CostEstimate(flops=0, bytes_accessed=nbytes, transcendentals=0),
        name=name,
    )(*operands)


def query_kernel(tokens_ref, weight_ref, out_ref):
    heads, _, head_dim = out_ref.shape
    part = mm(tokens_ref[...], weight_ref[...], NN).astype(BF16)
    for head in range(heads):
        out_ref[head] = part[:, head * head_dim : (head + 1) * head_dim]


def project_query(tokens, weight, heads):
    rows, width = tokens.shape
    return pl.pallas_call(
        query_kernel,
        out_shape=pltpu.VMEM((heads, rows, width // heads), BF16),
        grid=(1,),
        in_specs=[pl.BlockSpec((rows, width), lambda i: (0, 0)), pl.BlockSpec((width, width), lambda i: (0, 0))],
        out_specs=pl.BlockSpec((heads, rows, width // heads), lambda i: (0, 0, 0)),
        compiler_params=pltpu.CompilerParams(vmem_limit_bytes=SMALL_LIMIT * 1024 * 1024),
        cost_estimate=pl.CostEstimate(flops=2 * rows * width * width, bytes_accessed=4 * width * (rows + width), transcendentals=0),
        name="query",
    )(*(pltpu.with_memory_space_constraint(x, pltpu.HBM) for x in (tokens, weight)))


def pair_sum_kernel(keep_ref, got_ref, *out_refs):
    for slot, out_ref in enumerate(out_refs):
        out_ref[...] = (keep_ref[slot].astype(F32) + got_ref[slot].astype(F32)).astype(BF16)


def up_sum_kernel(mine_ref, other_ref, out_ref):
    half = out_ref.shape[0]
    out_ref[...] = (mine_ref[:half].astype(F32) + other_ref[:half].astype(F32)).astype(BF16)


def sum_kernel(*refs):
    *parts, out_ref = refs
    total = parts[0][...].astype(F32)
    for part in parts[1:]:
        total = total + part[...].astype(F32)
    out_ref[...] = total.astype(BF16)


def stepped(totals, bases):
    norms = [jnp.sqrt(jnp.sum(total * total)) for total in totals]
    iterates = [(total / (norm + 1e-07)).astype(BF16) for total, norm in zip(totals, norms)]
    for step in range(NS_STEPS):
        grams = [mm(x, x, NT).astype(BF16) for x in iterates]
        squares = [mm(g, g, NN) for g in grams]
        mixers = [(coef_b * g.astype(F32) + coef_c * s).astype(BF16) for g, s in zip(grams, squares)]
        moved = [mm(m, x, NN) for m, x in zip(mixers, iterates)]
        iterates = [(coef_a * x.astype(F32) + y).astype(BF16) for x, y in zip(iterates, moved)]
    return [(base - step_size * x.astype(F32)).astype(BF16) for base, x in zip(bases, iterates)]


def newton_kernel(
    heads, first_ref, first_other_ref, second_ref, second_other_ref, half_ref, got_ref, base_ref, base_up_ref, out_ref, *part_refs
):
    half = half_ref.shape[0]
    even = position(heads)[1] == 0
    a, b = half_ref[...], got_ref[...]
    upper = jnp.concatenate([jnp.where(even, a, b), jnp.where(even, b, a)], axis=0).astype(F32)
    first = first_ref[half:].astype(F32) + first_other_ref[half:].astype(F32)
    second = second_ref[...].astype(F32) + second_other_ref[...].astype(F32)
    main, upper = stepped((jnp.concatenate([first, second], axis=0), upper), (base_ref[...], base_up_ref[...]))
    whole = jnp.concatenate([jnp.where(even, upper[:half], upper[half:]), main], axis=0)
    out_ref[...] = whole
    rows = whole.shape[0] // len(part_refs)
    for index, part_ref in enumerate(part_refs):
        part_ref[...] = whole[index * rows : (index + 1) * rows]


def head_output(even, q, here, there):
    head_dim = q.shape[1]
    here, there = (jnp.concatenate([ref[...] for ref in refs], axis=0) for refs in (here, there))
    a, b = jnp.where(even, here, there), jnp.where(even, there, here)
    half = head_dim // 2
    up_b = jnp.concatenate([a[:half], b[:half]], axis=0)
    gate = mm(q, a[half:], NN)
    upper = mm(q, up_b, NN)
    hidden = (gate * jax.nn.sigmoid(gate) * upper).astype(BF16)
    return mm(hidden, b[half:], NT).astype(BF16)


def apply_kernel(far, q_ref, *refs):
    *block_refs, out_ref = refs
    half = len(block_refs) // 2
    own, core = position(q_ref.shape[0])
    out_ref[...] = head_output(core == 0, q_ref[own ^ far], block_refs[:half], block_refs[half:])


def finish_kernel(q_ref, *refs):
    *piece_refs, first_ref, second_ref, first_there_ref, second_there_ref, out_hbm, pieces, whole, sems = refs
    heads, rows, head_dim = q_ref.shape
    own, core = position(heads)
    lot = rows // FINISH_LOTS
    copies = []
    for index in range(FINISH_LOTS):
        part = pl.ds(index * lot, lot)
        for far, piece_ref in enumerate(piece_refs):
            pieces[far, part] = piece_ref[part]
        q = q_ref[own ^ (heads - 1), part]
        pieces[heads - 1, part] = head_output(core == 0, q, (first_ref, second_ref), (first_there_ref, second_there_ref))
        for head in range(heads):
            whole[part, head * head_dim : (head + 1) * head_dim] = pieces[own ^ head, part]
        copies.append(pltpu.make_async_copy(whole.at[part], out_hbm.at[part], sems.at[index]))
        copies[-1].start()
    for copy in copies:
        copy.wait()


def finish(query, pieces, blocks):
    heads, rows, head_dim = query.shape
    operands = [pltpu.with_memory_space_constraint(x, pltpu.VMEM) for x in (query, *pieces, *blocks)]
    return pl.pallas_call(
        finish_kernel,
        out_shape=jax.ShapeDtypeStruct((rows, heads * head_dim), BF16),
        in_specs=[pl.BlockSpec(memory_space=pltpu.VMEM)] * len(operands),
        out_specs=pl.BlockSpec(memory_space=pl.ANY),
        scratch_shapes=[
            pltpu.VMEM((heads, rows, head_dim), BF16),
            pltpu.VMEM((rows, heads * head_dim), BF16),
            pltpu.SemaphoreType.DMA((FINISH_LOTS,)),
        ],
        compiler_params=pltpu.CompilerParams(vmem_limit_bytes=SMALL_LIMIT * 1024 * 1024),
        name="finish",
    )(*operands)


def shards(tokens, qkv_weight, w_gate, w_up, w_down, view_kind):
    rows, width = tokens.shape
    heads, head_dim, hidden = w_gate.shape
    groups = lax.axis_size("tok")
    own, core = position(heads)
    w_down_t = jnp.transpose(w_down, (0, 2, 1))
    half = head_dim // 2
    shape = lambda *dims: pltpu.VMEM(dims, BF16)
    size = head_dim * hidden
    main_block, half_block = shape(head_dim, hidden), shape(half, hidden)
    size = head_dim * hidden

    def exchange(x, bits):
        return lax.ppermute(x, "tok", [(i, i ^ bits) for i in range(groups)])

    first, second, first_give, second_give = gradients(view_kind, tokens, qkv_weight, w_gate, w_up, w_down_t)
    block, part_block = shape(head_dim + half, hidden), shape((head_dim + half) // 2, hidden)
    first, second = (
        small(pair_sum_kernel, [part_block] * heads, (keep, exchange(give, 1)), 9 * keep.size, "pair_sum")
        for keep, give in ((first, first_give), (second, second_give))
    )
    first_on, second_on = exchange(first[3], 2), exchange(second[3], 4)
    first_in, second_in = exchange(first[1], 2), exchange(second[2], 4)
    first_on = exchange(small(sum_kernel, part_block, (first[2], first_on), 6 * size, "pass_sum"), 4)
    second_on = exchange(small(sum_kernel, part_block, (second[1], second_on), 6 * size, "pass_sum"), 2)
    first = small(sum_kernel, part_block, (first[0], first_in, first_on), 8 * size, "plane_sum")
    second = small(sum_kernel, part_block, (second[0], second_in, second_on), 8 * size, "plane_sum")
    query = project_query(tokens, qkv_weight, heads)
    base = jnp.where(core == 0, lax.dynamic_index_in_dim(w_gate, own, 0, False), lax.dynamic_index_in_dim(w_down_t, own, 0, False))
    base_up = lax.dynamic_index_in_dim(w_up, own, 0, False)

    def over_line(total, name):
        bits = 2 * heads
        while bits < groups // 2:
            total = small(sum_kernel, shape(*total.shape), (total, exchange(total, bits)), 6 * total.size, name)
            bits *= 2
        return total, exchange(total, bits)

    first, first_other = over_line(first, "line_sum")
    second, second_other = over_line(second, "line_sum")
    first_other, query, base, base_up = lax.optimization_barrier((first_other, query, base, base_up))
    upper = small(up_sum_kernel, half_block, (first, first_other), 6 * size, "up_sum")
    args = (first, first_other, second, second_other, upper, exchange(upper, 1), base, base_up)
    kernel = functools.partial(newton_kernel, heads)
    fresh, first, second = small(kernel, [block, part_block, part_block], args, 30 * size, "newton")

    def apply(far, *args):
        return small(functools.partial(apply_kernel, far), shape(rows, head_dim), (query, *args), 20 * rows * head_dim, "apply")

    over_y, over_z = [exchange(x, 2) for x in (first, second)], [exchange(x, 4) for x in (first, second)]
    across = [exchange(over_y[0], 4), exchange(over_z[1], 2)]
    swapped = lambda blocks: (*blocks, *(exchange(x, 1) for x in blocks))
    piece = apply(0, fresh, exchange(fresh, 1))
    over_y, over_z, piece = lax.optimization_barrier((over_y, over_z, piece))
    pieces = [piece, apply(1, *swapped(over_y)), apply(2, *swapped(over_z))]
    return finish(query, pieces, swapped(across))


def solution(mesh):
    placed = (P(("scene", "tok"), None), P(), P(), P(), P(), P("scene"))
    return jax.shard_map(
        shards, mesh=mesh, in_specs=placed, out_specs=P(("scene", "tok"), None), check_vma=False
    )
```

```python
import functools

import jax
import jax.numpy as jnp
from jax import lax
from jax.experimental import pallas as pl
from jax.experimental.pallas import tpu as pltpu
from jax.sharding import PartitionSpec as P

VIEWS = 16
NS_STEPS = 5
BF16 = jnp.bfloat16
F32 = jnp.float32
K1_LIMIT = 40
SMALL_LIMIT = 24
FINISH_LOTS = 2

coef_a = 3.4445
coef_b = -4.775
coef_c = 2.0315
step_size = 0.8


def mm(a, b, dims):
    return lax.dot_general(a, b, (dims, ((), ())), preferred_element_type=F32)


NN = ((1,), (0,))
NT = ((1,), (1,))
TN = ((0,), (0,))


def position(heads):
    place = lax.axis_index("tok")
    return lax.rem(lax.div(place, 2), heads), lax.rem(place, 2)


def grad_kernel(
    view_hbm, tok_hbm, qkv_hbm, gate_hbm, up_hbm, down_hbm, first_keep_ref, second_keep_ref, first_give_ref, second_give_ref, view, tok, wkv, fast, kv, both_w, down_w, sems
):
    rows, width = tok.shape
    heads, head_dim = kv.shape[1], kv.shape[3]
    hidden = down_w.shape[2]
    half = head_dim // 2
    own, core = position(heads)
    owner = lax.div(lax.axis_index("tok") * rows, rows * lax.axis_size("tok") // VIEWS)
    count = iter(range(4 + 3 * heads))

    def fetch(source, target):
        copy = pltpu.make_async_copy(source, target, sems.at[next(count)])
        copy.start()
        return copy

    tok_copy = fetch(tok_hbm, tok)
    kv_copies = [fetch(qkv_hbm.at[:, (1 + which) * width : (2 + which) * width], wkv.at[which]) for which in range(2)]
    view_copy = fetch(view_hbm, view)
    fast_copies = [
        fetch(ref.at[head], fast.at[head, i]) for head in range(heads) for i, ref in enumerate((gate_hbm, up_hbm, down_hbm))
    ]
    tok_copy.wait()
    view_copy.wait()
    flag = view[owner].astype(F32)
    for which in range(2):
        kv_copies[which].wait()
        for pair in range(heads // 2):
            columns = slice(2 * pair * head_dim, (2 * pair + 2) * head_dim)
            part = mm(tok[...], wkv[which, :, columns], NN)
            part = (part * flag if which == 1 else part).astype(BF16)
            kv[which, 2 * pair] = part[:, :head_dim]
            kv[which, 2 * pair + 1] = part[:, head_dim:]
    for copy in fast_copies:
        copy.wait()
    for head in range(heads):
        both_w[head, :, :hidden] = fast[head, 0].astype(BF16)
        both_w[head, :, hidden:] = fast[head, 1].astype(BF16)
        down_w[head] = (-fast[head, 2]).astype(BF16)
    even = core == 0
    chunk = rows
    for head in range(heads):
        both_sum = down_sum = None
        for start in range(0, rows, chunk):
            k = kv[0, head, start : start + chunk, :]
            v = kv[1, head, start : start + chunk, :]
            both = mm(k, both_w[head], NN)
            dhid = mm(v, down_w[head], NN)
            gate, upper = both[:, :hidden], both[:, hidden:]
            sig = jax.nn.sigmoid(gate)
            act = gate * sig
            hid = (act * upper).astype(BF16)
            dgate = (dhid * upper * (sig + act * (1.0 - sig))).astype(BF16)
            dup = (dhid * act).astype(BF16)
            both_part = mm(k, jnp.concatenate([dgate, dup], axis=1), TN)
            down_part = mm(v, hid, TN)
            both_sum = both_part if both_sum is None else both_sum + both_part
            down_sum = down_part if down_sum is None else down_sum + down_part
        gate_g = both_sum[:, :hidden].astype(BF16)
        up_g = both_sum[:, hidden:].astype(BF16)
        down_g = (-down_sum).astype(BF16)
        slot = own ^ head
        keep = jnp.concatenate([jnp.where(even, up_g[:half], up_g[half:]), jnp.where(even, gate_g, down_g)], axis=0)
        give = jnp.concatenate([jnp.where(even, up_g[half:], up_g[:half]), jnp.where(even, down_g, gate_g)], axis=0)
        cut = keep.shape[0] // 2
        first_keep_ref[slot], second_keep_ref[slot] = keep[:cut], keep[cut:]
        first_give_ref[slot], second_give_ref[slot] = give[:cut], give[cut:]


def gradients(view_kind, tokens, qkv_weight, w_gate, w_up, w_down_t):
    rows, width = tokens.shape
    heads, head_dim, hidden = w_gate.shape
    args = [pltpu.with_memory_space_constraint(x, pltpu.HBM) for x in (view_kind, tokens, qkv_weight, w_gate, w_up, w_down_t)]
    shape = pltpu.VMEM((heads, head_dim * 3 // 4, hidden), BF16)
    return pl.pallas_call(
        grad_kernel,
        out_shape=[shape] * 4,
        in_specs=[pl.BlockSpec(memory_space=pl.ANY)] * 6,
        out_specs=[pl.BlockSpec(memory_space=pltpu.VMEM)] * 4,
        scratch_shapes=[
            pltpu.SMEM(view_kind.shape, jnp.int32),
            pltpu.VMEM((rows, width), BF16),
            pltpu.VMEM((2, width, width), BF16),
            pltpu.VMEM((heads, 3, head_dim, hidden), F32),
            pltpu.VMEM((2, heads, rows, head_dim), BF16),
            pltpu.VMEM((heads, head_dim, 2 * hidden), BF16),
            pltpu.VMEM((heads, head_dim, hidden), BF16),
            pltpu.SemaphoreType.DMA((4 + 3 * heads,)),
        ],
        compiler_params=pltpu.CompilerParams(vmem_limit_bytes=K1_LIMIT * 1024 * 1024),
        cost_estimate=pl.CostEstimate(
            flops=4 * rows * width * width + 12 * heads * rows * head_dim * hidden,
            bytes_accessed=2 * rows * width + 4 * width * width + 12 * heads * head_dim * hidden,
            transcendentals=heads * rows * hidden,
        ),
        name="gradients",
    )(*args)


def small(kernel, shapes, operands, nbytes, name):
    specs = [pl.BlockSpec(memory_space=pltpu.VMEM)] * len(operands)
    operands = [pltpu.with_memory_space_constraint(x, pltpu.VMEM) for x in operands]
    return pl.pallas_call(
        kernel,
        out_shape=shapes,
        in_specs=specs,
        compiler_params=pltpu.CompilerParams(vmem_limit_bytes=SMALL_LIMIT * 1024 * 1024),
        cost_estimate=pl.CostEstimate(flops=0, bytes_accessed=nbytes, transcendentals=0),
        name=name,
    )(*operands)


def query_kernel(tokens_ref, weight_ref, out_ref):
    heads, _, head_dim = out_ref.shape
    part = mm(tokens_ref[...], weight_ref[...], NN).astype(BF16)
    for head in range(heads):
        out_ref[head] = part[:, head * head_dim : (head + 1) * head_dim]


def project_query(tokens, weight, heads):
    rows, width = tokens.shape
    return pl.pallas_call(
        query_kernel,
        out_shape=pltpu.VMEM((heads, rows, width // heads), BF16),
        grid=(1,),
        in_specs=[pl.BlockSpec((rows, width), lambda i: (0, 0)), pl.BlockSpec((width, width), lambda i: (0, 0))],
        out_specs=pl.BlockSpec((heads, rows, width // heads), lambda i: (0, 0, 0)),
        compiler_params=pltpu.CompilerParams(vmem_limit_bytes=SMALL_LIMIT * 1024 * 1024),
        cost_estimate=pl.CostEstimate(flops=2 * rows * width * width, bytes_accessed=4 * width * (rows + width), transcendentals=0),
        name="query",
    )(*(pltpu.with_memory_space_constraint(x, pltpu.HBM) for x in (tokens, weight)))


def pair_sum_kernel(keep_ref, got_ref, *out_refs):
    for slot, out_ref in enumerate(out_refs):
        out_ref[...] = (keep_ref[slot].astype(F32) + got_ref[slot].astype(F32)).astype(BF16)


def up_sum_kernel(mine_ref, other_ref, out_ref):
    half = out_ref.shape[0]
    out_ref[...] = (mine_ref[:half].astype(F32) + other_ref[:half].astype(F32)).astype(BF16)


def sum_kernel(*refs):
    *parts, out_ref = refs
    total = parts[0][...].astype(F32)
    for part in parts[1:]:
        total = total + part[...].astype(F32)
    out_ref[...] = total.astype(BF16)


def stepped(totals, bases):
    norms = [jnp.sqrt(jnp.sum(total * total)) for total in totals]
    iterates = [(total / (norm + 1e-07)).astype(BF16) for total, norm in zip(totals, norms)]
    for step in range(NS_STEPS):
        grams = [mm(x, x, NT).astype(BF16) for x in iterates]
        squares = [mm(g, g, NN) for g in grams]
        mixers = [(coef_b * g.astype(F32) + coef_c * s).astype(BF16) for g, s in zip(grams, squares)]
        moved = [mm(m, x, NN) for m, x in zip(mixers, iterates)]
        iterates = [(coef_a * x.astype(F32) + y).astype(BF16) for x, y in zip(iterates, moved)]
    return [(base - step_size * x.astype(F32)).astype(BF16) for base, x in zip(bases, iterates)]


def newton_kernel(
    heads, first_ref, first_other_ref, second_ref, second_other_ref, half_ref, got_ref, base_ref, base_up_ref, out_ref, *part_refs
):
    half = half_ref.shape[0]
    even = position(heads)[1] == 0
    a, b = half_ref[...], got_ref[...]
    upper = jnp.concatenate([jnp.where(even, a, b), jnp.where(even, b, a)], axis=0).astype(F32)
    first = first_ref[half:].astype(F32) + first_other_ref[half:].astype(F32)
    second = second_ref[...].astype(F32) + second_other_ref[...].astype(F32)
    main, upper = stepped((jnp.concatenate([first, second], axis=0), upper), (base_ref[...], base_up_ref[...]))
    whole = jnp.concatenate([jnp.where(even, upper[:half], upper[half:]), main], axis=0)
    out_ref[...] = whole
    rows = whole.shape[0] // len(part_refs)
    for index, part_ref in enumerate(part_refs):
        part_ref[...] = whole[index * rows : (index + 1) * rows]


def head_output(even, q, here, there):
    head_dim = q.shape[1]
    here, there = (jnp.concatenate([ref[...] for ref in refs], axis=0) for refs in (here, there))
    a, b = jnp.where(even, here, there), jnp.where(even, there, here)
    half = head_dim // 2
    up_b = jnp.concatenate([a[:half], b[:half]], axis=0)
    gate = mm(q, a[half:], NN)
    upper = mm(q, up_b, NN)
    hidden = (gate * jax.nn.sigmoid(gate) * upper).astype(BF16)
    return mm(hidden, b[half:], NT).astype(BF16)


def apply_kernel(far, q_ref, *refs):
    *block_refs, out_ref = refs
    half = len(block_refs) // 2
    own, core = position(q_ref.shape[0])
    out_ref[...] = head_output(core == 0, q_ref[own ^ far], block_refs[:half], block_refs[half:])


def apply_two_kernel(q_ref, *refs):
    *block_refs, near_ref, far_ref = refs
    count = len(block_refs) // 4
    own, core = position(q_ref.shape[0])
    lots = [block_refs[i * count : (i + 1) * count] for i in range(4)]
    near_ref[...] = head_output(core == 0, q_ref[own ^ 1], lots[0], lots[1])
    far_ref[...] = head_output(core == 0, q_ref[own ^ 2], lots[2], lots[3])


def finish_kernel(q_ref, *refs):
    *piece_refs, first_ref, second_ref, first_there_ref, second_there_ref, out_hbm, pieces, whole, sems = refs
    heads, rows, head_dim = q_ref.shape
    own, core = position(heads)
    lot = rows // FINISH_LOTS
    copies = []
    for index in range(FINISH_LOTS):
        part = pl.ds(index * lot, lot)
        for far, piece_ref in enumerate(piece_refs):
            pieces[far, part] = piece_ref[part]
        q = q_ref[own ^ (heads - 1), part]
        pieces[heads - 1, part] = head_output(core == 0, q, (first_ref, second_ref), (first_there_ref, second_there_ref))
        for head in range(heads):
            whole[part, head * head_dim : (head + 1) * head_dim] = pieces[own ^ head, part]
        copies.append(pltpu.make_async_copy(whole.at[part], out_hbm.at[part], sems.at[index]))
        copies[-1].start()
    for copy in copies:
        copy.wait()


def finish(query, pieces, blocks):
    heads, rows, head_dim = query.shape
    operands = [pltpu.with_memory_space_constraint(x, pltpu.VMEM) for x in (query, *pieces, *blocks)]
    return pl.pallas_call(
        finish_kernel,
        out_shape=jax.ShapeDtypeStruct((rows, heads * head_dim), BF16),
        in_specs=[pl.BlockSpec(memory_space=pltpu.VMEM)] * len(operands),
        out_specs=pl.BlockSpec(memory_space=pl.ANY),
        scratch_shapes=[
            pltpu.VMEM((heads, rows, head_dim), BF16),
            pltpu.VMEM((rows, heads * head_dim), BF16),
            pltpu.SemaphoreType.DMA((FINISH_LOTS,)),
        ],
        compiler_params=pltpu.CompilerParams(vmem_limit_bytes=SMALL_LIMIT * 1024 * 1024),
        name="finish",
    )(*operands)


def shards(tokens, qkv_weight, w_gate, w_up, w_down, view_kind):
    rows, width = tokens.shape
    heads, head_dim, hidden = w_gate.shape
    groups = lax.axis_size("tok")
    own, core = position(heads)
    w_down_t = jnp.transpose(w_down, (0, 2, 1))
    half = head_dim // 2
    shape = lambda *dims: pltpu.VMEM(dims, BF16)
    size = head_dim * hidden
    main_block, half_block = shape(head_dim, hidden), shape(half, hidden)
    size = head_dim * hidden

    def exchange(x, bits):
        return lax.ppermute(x, "tok", [(i, i ^ bits) for i in range(groups)])

    first, second, first_give, second_give = gradients(view_kind, tokens, qkv_weight, w_gate, w_up, w_down_t)
    block, part_block = shape(head_dim + half, hidden), shape((head_dim + half) // 2, hidden)
    first, second = (
        small(pair_sum_kernel, [part_block] * heads, (keep, exchange(give, 1)), 9 * keep.size, "pair_sum")
        for keep, give in ((first, first_give), (second, second_give))
    )
    first_on, second_on = exchange(first[3], 2), exchange(second[3], 4)
    first_in, second_in = exchange(first[1], 2), exchange(second[2], 4)
    first_on = exchange(small(sum_kernel, part_block, (first[2], first_on), 6 * size, "pass_sum"), 4)
    second_on = exchange(small(sum_kernel, part_block, (second[1], second_on), 6 * size, "pass_sum"), 2)
    first = small(sum_kernel, part_block, (first[0], first_in, first_on), 8 * size, "plane_sum")
    second = small(sum_kernel, part_block, (second[0], second_in, second_on), 8 * size, "plane_sum")
    query = project_query(tokens, qkv_weight, heads)
    base = jnp.where(core == 0, lax.dynamic_index_in_dim(w_gate, own, 0, False), lax.dynamic_index_in_dim(w_down_t, own, 0, False))
    base_up = lax.dynamic_index_in_dim(w_up, own, 0, False)

    def over_line(total, name):
        bits = 2 * heads
        while bits < groups // 2:
            total = small(sum_kernel, shape(*total.shape), (total, exchange(total, bits)), 6 * total.size, name)
            bits *= 2
        return total, exchange(total, bits)

    first, first_other = over_line(first, "line_sum")
    second, second_other = over_line(second, "line_sum")
    first_other, query, base, base_up = lax.optimization_barrier((first_other, query, base, base_up))
    upper = small(up_sum_kernel, half_block, (first, first_other), 6 * size, "up_sum")
    args = (first, first_other, second, second_other, upper, exchange(upper, 1), base, base_up)
    kernel = functools.partial(newton_kernel, heads)
    fresh, first, second = small(kernel, [block, part_block, part_block], args, 30 * size, "newton")

    def apply(far, *args):
        return small(functools.partial(apply_kernel, far), shape(rows, head_dim), (query, *args), 20 * rows * head_dim, "apply")

    over_y, over_z = [exchange(x, 2) for x in (first, second)], [exchange(x, 4) for x in (first, second)]
    across = [exchange(over_y[0], 4), exchange(over_z[1], 2)]
    swapped = lambda blocks: (*blocks, *(exchange(x, 1) for x in blocks))
    piece = apply(0, fresh, exchange(fresh, 1))
    over_y, over_z, piece = lax.optimization_barrier((over_y, over_z, piece))
    args = (query, *swapped(over_y), *swapped(over_z))
    pieces = [piece, *small(apply_two_kernel, [shape(rows, head_dim)] * 2, args, 40 * rows * head_dim, "apply_two")]
    return finish(query, pieces, swapped(across))


def solution(mesh):
    placed = (P(("scene", "tok"), None), P(), P(), P(), P(), P("scene"))
    return jax.shard_map(
        shards, mesh=mesh, in_specs=placed, out_specs=P(("scene", "tok"), None), check_vma=False
    )
```

```python
import functools

import jax
import jax.numpy as jnp
from jax import lax
from jax.experimental import pallas as pl
from jax.experimental.pallas import tpu as pltpu
from jax.sharding import PartitionSpec as P

VIEWS = 16
NS_STEPS = 5
BF16 = jnp.bfloat16
F32 = jnp.float32
K1_LIMIT = 40
SMALL_LIMIT = 24
FINISH_LOTS = 2

coef_a = 3.4445
coef_b = -4.775
coef_c = 2.0315
step_size = 0.8


def mm(a, b, dims):
    return lax.dot_general(a, b, (dims, ((), ())), preferred_element_type=F32)


NN = ((1,), (0,))
NT = ((1,), (1,))
TN = ((0,), (0,))


def position(heads):
    place = lax.axis_index("tok")
    return lax.rem(lax.div(place, 2), heads), lax.rem(place, 2)


def grad_kernel(
    view_hbm, tok_hbm, qkv_hbm, gate_hbm, up_hbm, down_hbm, first_keep_ref, second_keep_ref, first_give_ref, second_give_ref, view, tok, wkv, fast, kv, both_w, down_w, sems
):
    rows, width = tok.shape
    heads, head_dim = kv.shape[1], kv.shape[3]
    hidden = down_w.shape[2]
    half = head_dim // 2
    own, core = position(heads)
    owner = lax.div(lax.axis_index("tok") * rows, rows * lax.axis_size("tok") // VIEWS)
    count = iter(range(4 + 3 * heads))

    def fetch(source, target):
        copy = pltpu.make_async_copy(source, target, sems.at[next(count)])
        copy.start()
        return copy

    tok_copy = fetch(tok_hbm, tok)
    kv_copies = [fetch(qkv_hbm.at[:, (1 + which) * width : (2 + which) * width], wkv.at[which]) for which in range(2)]
    view_copy = fetch(view_hbm, view)
    fast_copies = [
        fetch(ref.at[head], fast.at[head, i]) for head in range(heads) for i, ref in enumerate((gate_hbm, up_hbm, down_hbm))
    ]
    tok_copy.wait()
    view_copy.wait()
    flag = view[owner].astype(F32)
    for which in range(2):
        kv_copies[which].wait()
        for pair in range(heads // 2):
            columns = slice(2 * pair * head_dim, (2 * pair + 2) * head_dim)
            part = mm(tok[...], wkv[which, :, columns], NN)
            part = (part * flag if which == 1 else part).astype(BF16)
            kv[which, 2 * pair] = part[:, :head_dim]
            kv[which, 2 * pair + 1] = part[:, head_dim:]
    for copy in fast_copies:
        copy.wait()
    for head in range(heads):
        both_w[head, :, :hidden] = fast[head, 0].astype(BF16)
        both_w[head, :, hidden:] = fast[head, 1].astype(BF16)
        down_w[head] = (-fast[head, 2]).astype(BF16)
    even = core == 0
    chunk = rows
    for head in range(heads):
        both_sum = down_sum = None
        for start in range(0, rows, chunk):
            k = kv[0, head, start : start + chunk, :]
            v = kv[1, head, start : start + chunk, :]
            both = mm(k, both_w[head], NN)
            dhid = mm(v, down_w[head], NN)
            gate, upper = both[:, :hidden], both[:, hidden:]
            sig = jax.nn.sigmoid(gate)
            act = gate * sig
            hid = (act * upper).astype(BF16)
            dgate = (dhid * upper * (sig + act * (1.0 - sig))).astype(BF16)
            dup = (dhid * act).astype(BF16)
            both_part = mm(k, jnp.concatenate([dgate, dup], axis=1), TN)
            down_part = mm(v, hid, TN)
            both_sum = both_part if both_sum is None else both_sum + both_part
            down_sum = down_part if down_sum is None else down_sum + down_part
        gate_g = both_sum[:, :hidden].astype(BF16)
        up_g = both_sum[:, hidden:].astype(BF16)
        down_g = (-down_sum).astype(BF16)
        slot = own ^ head
        keep = jnp.concatenate([jnp.where(even, up_g[:half], up_g[half:]), jnp.where(even, gate_g, down_g)], axis=0)
        give = jnp.concatenate([jnp.where(even, up_g[half:], up_g[:half]), jnp.where(even, down_g, gate_g)], axis=0)
        cut = keep.shape[0] // 2
        first_keep_ref[slot], second_keep_ref[slot] = keep[:cut], keep[cut:]
        first_give_ref[slot], second_give_ref[slot] = give[:cut], give[cut:]


def gradients(view_kind, tokens, qkv_weight, w_gate, w_up, w_down_t):
    rows, width = tokens.shape
    heads, head_dim, hidden = w_gate.shape
    args = [pltpu.with_memory_space_constraint(x, pltpu.HBM) for x in (view_kind, tokens, qkv_weight, w_gate, w_up, w_down_t)]
    shape = pltpu.VMEM((heads, head_dim * 3 // 4, hidden), BF16)
    return pl.pallas_call(
        grad_kernel,
        out_shape=[shape] * 4,
        in_specs=[pl.BlockSpec(memory_space=pl.ANY)] * 6,
        out_specs=[pl.BlockSpec(memory_space=pltpu.VMEM)] * 4,
        scratch_shapes=[
            pltpu.SMEM(view_kind.shape, jnp.int32),
            pltpu.VMEM((rows, width), BF16),
            pltpu.VMEM((2, width, width), BF16),
            pltpu.VMEM((heads, 3, head_dim, hidden), F32),
            pltpu.VMEM((2, heads, rows, head_dim), BF16),
            pltpu.VMEM((heads, head_dim, 2 * hidden), BF16),
            pltpu.VMEM((heads, head_dim, hidden), BF16),
            pltpu.SemaphoreType.DMA((4 + 3 * heads,)),
        ],
        compiler_params=pltpu.CompilerParams(vmem_limit_bytes=K1_LIMIT * 1024 * 1024),
        cost_estimate=pl.CostEstimate(
            flops=4 * rows * width * width + 12 * heads * rows * head_dim * hidden,
            bytes_accessed=2 * rows * width + 4 * width * width + 12 * heads * head_dim * hidden,
            transcendentals=heads * rows * hidden,
        ),
        name="gradients",
    )(*args)


def small(kernel, shapes, operands, nbytes, name):
    specs = [pl.BlockSpec(memory_space=pltpu.VMEM)] * len(operands)
    operands = [pltpu.with_memory_space_constraint(x, pltpu.VMEM) for x in operands]
    return pl.pallas_call(
        kernel,
        out_shape=shapes,
        in_specs=specs,
        compiler_params=pltpu.CompilerParams(vmem_limit_bytes=SMALL_LIMIT * 1024 * 1024),
        cost_estimate=pl.CostEstimate(flops=0, bytes_accessed=nbytes, transcendentals=0),
        name=name,
    )(*operands)


def query_kernel(tokens_ref, weight_ref, out_ref):
    heads, _, head_dim = out_ref.shape
    part = mm(tokens_ref[...], weight_ref[...], NN).astype(BF16)
    for head in range(heads):
        out_ref[head] = part[:, head * head_dim : (head + 1) * head_dim]


def project_query(tokens, weight, heads):
    rows, width = tokens.shape
    return pl.pallas_call(
        query_kernel,
        out_shape=pltpu.VMEM((heads, rows, width // heads), BF16),
        grid=(1,),
        in_specs=[pl.BlockSpec((rows, width), lambda i: (0, 0)), pl.BlockSpec((width, width), lambda i: (0, 0))],
        out_specs=pl.BlockSpec((heads, rows, width // heads), lambda i: (0, 0, 0)),
        compiler_params=pltpu.CompilerParams(vmem_limit_bytes=SMALL_LIMIT * 1024 * 1024),
        cost_estimate=pl.CostEstimate(flops=2 * rows * width * width, bytes_accessed=4 * width * (rows + width), transcendentals=0),
        name="query",
    )(*(pltpu.with_memory_space_constraint(x, pltpu.HBM) for x in (tokens, weight)))


def pair_sum_kernel(keep_ref, got_ref, *out_refs):
    for slot, out_ref in enumerate(out_refs):
        out_ref[...] = (keep_ref[slot].astype(F32) + got_ref[slot].astype(F32)).astype(BF16)


def up_sum_kernel(mine_ref, other_ref, out_ref):
    half = out_ref.shape[0]
    out_ref[...] = (mine_ref[:half].astype(F32) + other_ref[:half].astype(F32)).astype(BF16)


def sum_kernel(*refs):
    *parts, out_ref = refs
    total = parts[0][...].astype(F32)
    for part in parts[1:]:
        total = total + part[...].astype(F32)
    out_ref[...] = total.astype(BF16)


def stepped(totals, bases):
    norms = [jnp.sqrt(jnp.sum(total * total)) for total in totals]
    iterates = [(total / (norm + 1e-07)).astype(BF16) for total, norm in zip(totals, norms)]
    for step in range(NS_STEPS):
        grams = [mm(x, x, NT).astype(BF16) for x in iterates]
        squares = [mm(g, g, NN) for g in grams]
        mixers = [(coef_b * g.astype(F32) + coef_c * s).astype(BF16) for g, s in zip(grams, squares)]
        moved = [mm(m, x, NN) for m, x in zip(mixers, iterates)]
        iterates = [(coef_a * x.astype(F32) + y).astype(BF16) for x, y in zip(iterates, moved)]
    return [(base - step_size * x.astype(F32)).astype(BF16) for base, x in zip(bases, iterates)]


def newton_kernel(
    heads, first_ref, first_other_ref, second_ref, second_other_ref, half_ref, got_ref, base_ref, base_up_ref, out_ref, *part_refs
):
    half = half_ref.shape[0]
    even = position(heads)[1] == 0
    a, b = half_ref[...], got_ref[...]
    upper = jnp.concatenate([jnp.where(even, a, b), jnp.where(even, b, a)], axis=0).astype(F32)
    first = first_ref[half:].astype(F32) + first_other_ref[half:].astype(F32)
    second = second_ref[...].astype(F32) + second_other_ref[...].astype(F32)
    main, upper = stepped((jnp.concatenate([first, second], axis=0), upper), (base_ref[...], base_up_ref[...]))
    whole = jnp.concatenate([jnp.where(even, upper[:half], upper[half:]), main], axis=0)
    out_ref[...] = whole
    rows = whole.shape[0] // len(part_refs)
    for index, part_ref in enumerate(part_refs):
        part_ref[...] = whole[index * rows : (index + 1) * rows]


def head_output(even, q, here, there):
    head_dim = q.shape[1]
    here, there = (jnp.concatenate([ref[...] for ref in refs], axis=0) for refs in (here, there))
    a, b = jnp.where(even, here, there), jnp.where(even, there, here)
    half = head_dim // 2
    up_b = jnp.concatenate([a[:half], b[:half]], axis=0)
    gate = mm(q, a[half:], NN)
    upper = mm(q, up_b, NN)
    hidden = (gate * jax.nn.sigmoid(gate) * upper).astype(BF16)
    return mm(hidden, b[half:], NT).astype(BF16)


def apply_kernel(far, q_ref, *refs):
    *block_refs, out_ref = refs
    half = len(block_refs) // 2
    own, core = position(q_ref.shape[0])
    out_ref[...] = head_output(core == 0, q_ref[own ^ far], block_refs[:half], block_refs[half:])


def beside(even_head, a, b):
    return jnp.concatenate([jnp.where(even_head, a, b), jnp.where(even_head, b, a)], axis=1)


def apply_two_kernel(q_ref, piece_ref, *refs):
    *block_refs, pair_ref, far_ref = refs
    count = len(block_refs) // 4
    own, core = position(q_ref.shape[0])
    lots = [block_refs[i * count : (i + 1) * count] for i in range(4)]
    near = head_output(core == 0, q_ref[own ^ 1], lots[0], lots[1])
    pair_ref[...] = beside(lax.rem(own, 2) == 0, piece_ref[...], near)
    far_ref[...] = head_output(core == 0, q_ref[own ^ 2], lots[2], lots[3])


def finish_kernel(q_ref, pair_ref, far_ref, first_ref, second_ref, first_there_ref, second_there_ref, out_hbm, other, sems):
    heads, rows, head_dim = q_ref.shape
    own, core = position(heads)
    pair = lax.div(own, 2)
    lot = rows // FINISH_LOTS
    columns = [pl.ds(pl.multiple_of(p * 2 * head_dim, 128), 2 * head_dim) for p in (pair, pair ^ 1)]
    copies = [pltpu.make_async_copy(pair_ref, out_hbm.at[:, columns[0]], sems.at[FINISH_LOTS])]
    copies[0].start()
    for index in range(FINISH_LOTS):
        part = pl.ds(index * lot, lot)
        q = q_ref[own ^ (heads - 1), part]
        last = head_output(core == 0, q, (first_ref, second_ref), (first_there_ref, second_there_ref))
        other[part] = beside(lax.rem(own, 2) == 0, far_ref[part], last)
        copies.append(pltpu.make_async_copy(other.at[part], out_hbm.at[part, columns[1]], sems.at[index]))
        copies[-1].start()
    for copy in copies:
        copy.wait()


def finish(query, pieces, blocks):
    heads, rows, head_dim = query.shape
    operands = [pltpu.with_memory_space_constraint(x, pltpu.VMEM) for x in (query, *pieces, *blocks)]
    return pl.pallas_call(
        finish_kernel,
        out_shape=jax.ShapeDtypeStruct((rows, heads * head_dim), BF16),
        in_specs=[pl.BlockSpec(memory_space=pltpu.VMEM)] * len(operands),
        out_specs=pl.BlockSpec(memory_space=pl.ANY),
        scratch_shapes=[
            pltpu.VMEM((rows, 2 * head_dim), BF16),
            pltpu.SemaphoreType.DMA((FINISH_LOTS + 1,)),
        ],
        compiler_params=pltpu.CompilerParams(vmem_limit_bytes=SMALL_LIMIT * 1024 * 1024),
        name="finish",
    )(*operands)


def shards(tokens, qkv_weight, w_gate, w_up, w_down, view_kind):
    rows, width = tokens.shape
    heads, head_dim, hidden = w_gate.shape
    groups = lax.axis_size("tok")
    own, core = position(heads)
    w_down_t = jnp.transpose(w_down, (0, 2, 1))
    half = head_dim // 2
    shape = lambda *dims: pltpu.VMEM(dims, BF16)
    size = head_dim * hidden
    main_block, half_block = shape(head_dim, hidden), shape(half, hidden)
    size = head_dim * hidden

    def exchange(x, bits):
        return lax.ppermute(x, "tok", [(i, i ^ bits) for i in range(groups)])

    first, second, first_give, second_give = gradients(view_kind, tokens, qkv_weight, w_gate, w_up, w_down_t)
    block, part_block = shape(head_dim + half, hidden), shape((head_dim + half) // 2, hidden)
    first, second = (
        small(pair_sum_kernel, [part_block] * heads, (keep, exchange(give, 1)), 9 * keep.size, "pair_sum")
        for keep, give in ((first, first_give), (second, second_give))
    )
    first_on, second_on = exchange(first[3], 2), exchange(second[3], 4)
    first_in, second_in = exchange(first[1], 2), exchange(second[2], 4)
    first_on = exchange(small(sum_kernel, part_block, (first[2], first_on), 6 * size, "pass_sum"), 4)
    second_on = exchange(small(sum_kernel, part_block, (second[1], second_on), 6 * size, "pass_sum"), 2)
    first = small(sum_kernel, part_block, (first[0], first_in, first_on), 8 * size, "plane_sum")
    second = small(sum_kernel, part_block, (second[0], second_in, second_on), 8 * size, "plane_sum")
    query = project_query(tokens, qkv_weight, heads)
    base = jnp.where(core == 0, lax.dynamic_index_in_dim(w_gate, own, 0, False), lax.dynamic_index_in_dim(w_down_t, own, 0, False))
    base_up = lax.dynamic_index_in_dim(w_up, own, 0, False)

    def over_line(total, name):
        bits = 2 * heads
        while bits < groups // 2:
            total = small(sum_kernel, shape(*total.shape), (total, exchange(total, bits)), 6 * total.size, name)
            bits *= 2
        return total, exchange(total, bits)

    first, first_other = over_line(first, "line_sum")
    second, second_other = over_line(second, "line_sum")
    first_other, query, base, base_up = lax.optimization_barrier((first_other, query, base, base_up))
    upper = small(up_sum_kernel, half_block, (first, first_other), 6 * size, "up_sum")
    args = (first, first_other, second, second_other, upper, exchange(upper, 1), base, base_up)
    kernel = functools.partial(newton_kernel, heads)
    fresh, first, second = small(kernel, [block, part_block, part_block], args, 30 * size, "newton")

    def apply(far, *args):
        return small(functools.partial(apply_kernel, far), shape(rows, head_dim), (query, *args), 20 * rows * head_dim, "apply")

    over_y, over_z = [exchange(x, 2) for x in (first, second)], [exchange(x, 4) for x in (first, second)]
    across = [exchange(over_y[0], 4), exchange(over_z[1], 2)]
    swapped = lambda blocks: (*blocks, *(exchange(x, 1) for x in blocks))
    piece = apply(0, fresh, exchange(fresh, 1))
    over_y, over_z, piece = lax.optimization_barrier((over_y, over_z, piece))
    args = (query, piece, *swapped(over_y), *swapped(over_z))
    shapes = [shape(rows, 2 * head_dim), shape(rows, head_dim)]
    pieces = small(apply_two_kernel, shapes, args, 40 * rows * head_dim, "apply_two")
    return finish(query, pieces, swapped(across))


def solution(mesh):
    placed = (P(("scene", "tok"), None), P(), P(), P(), P(), P("scene"))
    return jax.shard_map(
        shards, mesh=mesh, in_specs=placed, out_specs=P(("scene", "tok"), None), check_vma=False
    )
```

```python
import functools

import jax
import jax.numpy as jnp
from jax import lax
from jax.experimental import pallas as pl
from jax.experimental.pallas import tpu as pltpu
from jax.sharding import PartitionSpec as P

VIEWS = 16
NS_STEPS = 5
BF16 = jnp.bfloat16
F32 = jnp.float32
K1_LIMIT = 40
SMALL_LIMIT = 24
FINISH_LOTS = 2

coef_a = 3.4445
coef_b = -4.775
coef_c = 2.0315
step_size = 0.8


def mm(a, b, dims):
    return lax.dot_general(a, b, (dims, ((), ())), preferred_element_type=F32)


NN = ((1,), (0,))
NT = ((1,), (1,))
TN = ((0,), (0,))


def position(heads):
    place = lax.axis_index("tok")
    return lax.rem(lax.div(place, 2), heads), lax.rem(place, 2)


def grad_kernel(
    view_hbm, tok_hbm, qkv_hbm, gate_hbm, up_hbm, down_hbm, first_keep_ref, second_keep_ref, first_give_ref, second_give_ref, view, tok, wkv, fast, kv, both_w, down_w, sems
):
    rows, width = tok.shape
    heads, head_dim = kv.shape[1], kv.shape[3]
    hidden = down_w.shape[2]
    half = head_dim // 2
    own, core = position(heads)
    owner = lax.div(lax.axis_index("tok") * rows, rows * lax.axis_size("tok") // VIEWS)
    count = iter(range(4 + 3 * heads))

    def fetch(source, target):
        copy = pltpu.make_async_copy(source, target, sems.at[next(count)])
        copy.start()
        return copy

    tok_copy = fetch(tok_hbm, tok)
    kv_copies = [fetch(qkv_hbm.at[:, (1 + which) * width : (2 + which) * width], wkv.at[which]) for which in range(2)]
    view_copy = fetch(view_hbm, view)
    fast_copies = [
        fetch(ref.at[head], fast.at[head, i]) for head in range(heads) for i, ref in enumerate((gate_hbm, up_hbm, down_hbm))
    ]
    tok_copy.wait()
    view_copy.wait()
    flag = view[owner].astype(F32)
    for which in range(2):
        kv_copies[which].wait()
        for pair in range(heads // 2):
            columns = slice(2 * pair * head_dim, (2 * pair + 2) * head_dim)
            part = mm(tok[...], wkv[which, :, columns], NN)
            part = (part * flag if which == 1 else part).astype(BF16)
            kv[which, 2 * pair] = part[:, :head_dim]
            kv[which, 2 * pair + 1] = part[:, head_dim:]
    for copy in fast_copies:
        copy.wait()
    for head in range(heads):
        both_w[head, :, :hidden] = fast[head, 0].astype(BF16)
        both_w[head, :, hidden:] = fast[head, 1].astype(BF16)
        down_w[head] = (-fast[head, 2]).astype(BF16)
    even = core == 0
    chunk = rows
    for head in range(heads):
        both_sum = down_sum = None
        for start in range(0, rows, chunk):
            k = kv[0, head, start : start + chunk, :]
            v = kv[1, head, start : start + chunk, :]
            both = mm(k, both_w[head], NN)
            dhid = mm(v, down_w[head], NN)
            gate, upper = both[:, :hidden], both[:, hidden:]
            sig = jax.nn.sigmoid(gate)
            act = gate * sig
            hid = (act * upper).astype(BF16)
            dgate = (dhid * upper * (sig + act * (1.0 - sig))).astype(BF16)
            dup = (dhid * act).astype(BF16)
            both_part = mm(k, jnp.concatenate([dgate, dup], axis=1), TN)
            down_part = mm(v, hid, TN)
            both_sum = both_part if both_sum is None else both_sum + both_part
            down_sum = down_part if down_sum is None else down_sum + down_part
        gate_g = both_sum[:, :hidden].astype(BF16)
        up_g = both_sum[:, hidden:].astype(BF16)
        down_g = (-down_sum).astype(BF16)
        slot = own ^ head
        keep = jnp.concatenate([jnp.where(even, up_g[:half], up_g[half:]), jnp.where(even, gate_g, down_g)], axis=0)
        give = jnp.concatenate([jnp.where(even, up_g[half:], up_g[:half]), jnp.where(even, down_g, gate_g)], axis=0)
        cut = keep.shape[0] // 2
        first_keep_ref[slot], second_keep_ref[slot] = keep[:cut], keep[cut:]
        first_give_ref[slot], second_give_ref[slot] = give[:cut], give[cut:]


def gradients(view_kind, tokens, qkv_weight, w_gate, w_up, w_down_t):
    rows, width = tokens.shape
    heads, head_dim, hidden = w_gate.shape
    args = [pltpu.with_memory_space_constraint(x, pltpu.HBM) for x in (view_kind, tokens, qkv_weight, w_gate, w_up, w_down_t)]
    shape = pltpu.VMEM((heads, head_dim * 3 // 4, hidden), BF16)
    return pl.pallas_call(
        grad_kernel,
        out_shape=[shape] * 4,
        in_specs=[pl.BlockSpec(memory_space=pl.ANY)] * 6,
        out_specs=[pl.BlockSpec(memory_space=pltpu.VMEM)] * 4,
        scratch_shapes=[
            pltpu.SMEM(view_kind.shape, jnp.int32),
            pltpu.VMEM((rows, width), BF16),
            pltpu.VMEM((2, width, width), BF16),
            pltpu.VMEM((heads, 3, head_dim, hidden), F32),
            pltpu.VMEM((2, heads, rows, head_dim), BF16),
            pltpu.VMEM((heads, head_dim, 2 * hidden), BF16),
            pltpu.VMEM((heads, head_dim, hidden), BF16),
            pltpu.SemaphoreType.DMA((4 + 3 * heads,)),
        ],
        compiler_params=pltpu.CompilerParams(vmem_limit_bytes=K1_LIMIT * 1024 * 1024),
        cost_estimate=pl.CostEstimate(
            flops=4 * rows * width * width + 12 * heads * rows * head_dim * hidden,
            bytes_accessed=2 * rows * width + 4 * width * width + 12 * heads * head_dim * hidden,
            transcendentals=heads * rows * hidden,
        ),
        name="gradients",
    )(*args)


def small(kernel, shapes, operands, nbytes, name):
    specs = [pl.BlockSpec(memory_space=pltpu.VMEM)] * len(operands)
    operands = [pltpu.with_memory_space_constraint(x, pltpu.VMEM) for x in operands]
    return pl.pallas_call(
        kernel,
        out_shape=shapes,
        in_specs=specs,
        compiler_params=pltpu.CompilerParams(vmem_limit_bytes=SMALL_LIMIT * 1024 * 1024),
        cost_estimate=pl.CostEstimate(flops=0, bytes_accessed=nbytes, transcendentals=0),
        name=name,
    )(*operands)


def query_kernel(tokens_ref, weight_ref, out_ref):
    heads, _, head_dim = out_ref.shape
    part = mm(tokens_ref[...], weight_ref[...], NN).astype(BF16)
    for head in range(heads):
        out_ref[head] = part[:, head * head_dim : (head + 1) * head_dim]


def project_query(tokens, weight, heads):
    rows, width = tokens.shape
    return pl.pallas_call(
        query_kernel,
        out_shape=pltpu.VMEM((heads, rows, width // heads), BF16),
        grid=(1,),
        in_specs=[pl.BlockSpec((rows, width), lambda i: (0, 0)), pl.BlockSpec((width, width), lambda i: (0, 0))],
        out_specs=pl.BlockSpec((heads, rows, width // heads), lambda i: (0, 0, 0)),
        compiler_params=pltpu.CompilerParams(vmem_limit_bytes=SMALL_LIMIT * 1024 * 1024),
        cost_estimate=pl.CostEstimate(flops=2 * rows * width * width, bytes_accessed=4 * width * (rows + width), transcendentals=0),
        name="query",
    )(*(pltpu.with_memory_space_constraint(x, pltpu.HBM) for x in (tokens, weight)))


def pair_sum_kernel(keep_ref, got_ref, *out_refs):
    for slot, out_ref in enumerate(out_refs):
        out_ref[...] = (keep_ref[slot].astype(F32) + got_ref[slot].astype(F32)).astype(BF16)


def up_sum_kernel(mine_ref, other_ref, out_ref):
    half = out_ref.shape[0]
    out_ref[...] = (mine_ref[:half].astype(F32) + other_ref[:half].astype(F32)).astype(BF16)


def sum_kernel(*refs):
    *parts, out_ref = refs
    total = parts[0][...].astype(F32)
    for part in parts[1:]:
        total = total + part[...].astype(F32)
    out_ref[...] = total.astype(BF16)


def stepped(totals, bases):
    norms = [jnp.sqrt(jnp.sum(total * total)) for total in totals]
    iterates = [(total / (norm + 1e-07)).astype(BF16) for total, norm in zip(totals, norms)]
    for step in range(NS_STEPS):
        grams = [mm(x, x, NT).astype(BF16) for x in iterates]
        squares = [mm(g, g, NN) for g in grams]
        mixers = [(coef_b * g.astype(F32) + coef_c * s).astype(BF16) for g, s in zip(grams, squares)]
        moved = [mm(m, x, NN) for m, x in zip(mixers, iterates)]
        iterates = [(coef_a * x.astype(F32) + y).astype(BF16) for x, y in zip(iterates, moved)]
    return [(base - step_size * x.astype(F32)).astype(BF16) for base, x in zip(bases, iterates)]


def newton_kernel(
    heads, first_ref, first_other_ref, second_ref, second_other_ref, half_ref, got_ref, base_ref, base_up_ref, out_ref, *part_refs
):
    half = half_ref.shape[0]
    even = position(heads)[1] == 0
    a, b = half_ref[...], got_ref[...]
    upper = jnp.concatenate([jnp.where(even, a, b), jnp.where(even, b, a)], axis=0).astype(F32)
    first = first_ref[half:].astype(F32) + first_other_ref[half:].astype(F32)
    second = second_ref[...].astype(F32) + second_other_ref[...].astype(F32)
    main, upper = stepped((jnp.concatenate([first, second], axis=0), upper), (base_ref[...], base_up_ref[...]))
    whole = jnp.concatenate([jnp.where(even, upper[:half], upper[half:]), main], axis=0)
    out_ref[...] = whole
    rows = whole.shape[0] // len(part_refs)
    for index, part_ref in enumerate(part_refs):
        part_ref[...] = whole[index * rows : (index + 1) * rows]


def head_output(even, q, here, there):
    head_dim = q.shape[1]
    here, there = (jnp.concatenate([ref[...] for ref in refs], axis=0) for refs in (here, there))
    a, b = jnp.where(even, here, there), jnp.where(even, there, here)
    half = head_dim // 2
    up_b = jnp.concatenate([a[:half], b[:half]], axis=0)
    gate = mm(q, a[half:], NN)
    upper = mm(q, up_b, NN)
    hidden = (gate * jax.nn.sigmoid(gate) * upper).astype(BF16)
    return mm(hidden, b[half:], NT).astype(BF16)


def apply_kernel(far, q_ref, *refs):
    *block_refs, out_ref = refs
    half = len(block_refs) // 2
    own, core = position(q_ref.shape[0])
    out_ref[...] = head_output(core == 0, q_ref[own ^ far], block_refs[:half], block_refs[half:])


def beside(even_head, a, b):
    return jnp.concatenate([jnp.where(even_head, a, b), jnp.where(even_head, b, a)], axis=1)


def apply_two_kernel(q_ref, piece_ref, *refs):
    *block_refs, pair_ref, far_ref = refs
    count = len(block_refs) // 4
    own, core = position(q_ref.shape[0])
    lots = [block_refs[i * count : (i + 1) * count] for i in range(4)]
    near = head_output(core == 0, q_ref[own ^ 1], lots[0], lots[1])
    pair_ref[...] = beside(lax.rem(own, 2) == 0, piece_ref[...], near)
    far_ref[...] = head_output(core == 0, q_ref[own ^ 2], lots[2], lots[3])


def finish_kernel(q_ref, pair_ref, far_ref, first_ref, second_ref, first_there_ref, second_there_ref, out_hbm, other, sems):
    heads, rows, head_dim = q_ref.shape
    own, core = position(heads)
    pair = lax.div(own, 2)
    lot = rows // FINISH_LOTS
    columns = [pl.ds(pl.multiple_of(p * 2 * head_dim, 128), 2 * head_dim) for p in (pair, pair ^ 1)]
    copies = [pltpu.make_async_copy(pair_ref, out_hbm.at[:, columns[0]], sems.at[FINISH_LOTS])]
    copies[0].start()
    for index in range(FINISH_LOTS):
        part = pl.ds(index * lot, lot)
        q = q_ref[own ^ (heads - 1), part]
        last = head_output(core == 0, q, (first_ref, second_ref), (first_there_ref, second_there_ref))
        other[part] = beside(lax.rem(own, 2) == 0, far_ref[part], last)
        copies.append(pltpu.make_async_copy(other.at[part], out_hbm.at[part, columns[1]], sems.at[index]))
        copies[-1].start()
    for copy in copies:
        copy.wait()


def finish(query, pieces, blocks):
    heads, rows, head_dim = query.shape
    operands = [pltpu.with_memory_space_constraint(x, pltpu.VMEM) for x in (query, *pieces, *blocks)]
    return pl.pallas_call(
        finish_kernel,
        out_shape=jax.ShapeDtypeStruct((rows, heads * head_dim), BF16),
        in_specs=[pl.BlockSpec(memory_space=pltpu.VMEM)] * len(operands),
        out_specs=pl.BlockSpec(memory_space=pl.ANY),
        scratch_shapes=[
            pltpu.VMEM((rows, 2 * head_dim), BF16),
            pltpu.SemaphoreType.DMA((FINISH_LOTS + 1,)),
        ],
        compiler_params=pltpu.CompilerParams(vmem_limit_bytes=SMALL_LIMIT * 1024 * 1024),
        name="finish",
    )(*operands)


def shards(tokens, qkv_weight, w_gate, w_up, w_down, view_kind):
    rows, width = tokens.shape
    heads, head_dim, hidden = w_gate.shape
    groups = lax.axis_size("tok")
    own, core = position(heads)
    w_down_t = jnp.transpose(w_down, (0, 2, 1))
    half = head_dim // 2
    shape = lambda *dims: pltpu.VMEM(dims, BF16)
    size = head_dim * hidden
    main_block, half_block = shape(head_dim, hidden), shape(half, hidden)
    size = head_dim * hidden

    def exchange(x, bits):
        return lax.ppermute(x, "tok", [(i, i ^ bits) for i in range(groups)])

    first, second, first_give, second_give = gradients(view_kind, tokens, qkv_weight, w_gate, w_up, w_down_t)
    block, part_block = shape(head_dim + half, hidden), shape((head_dim + half) // 2, hidden)
    first, second = (
        small(pair_sum_kernel, [part_block] * heads, (keep, exchange(give, 1)), 9 * keep.size, "pair_sum")
        for keep, give in ((first, first_give), (second, second_give))
    )
    first_on, second_on = exchange(first[3], 4), exchange(second[3], 2)
    first_in, second_in = exchange(first[2], 4), exchange(second[1], 2)
    first_on = exchange(small(sum_kernel, part_block, (first[1], first_on), 6 * size, "pass_sum"), 2)
    second_on = exchange(small(sum_kernel, part_block, (second[2], second_on), 6 * size, "pass_sum"), 4)
    first = small(sum_kernel, part_block, (first[0], first_in, first_on), 8 * size, "plane_sum")
    second = small(sum_kernel, part_block, (second[0], second_in, second_on), 8 * size, "plane_sum")
    query = project_query(tokens, qkv_weight, heads)
    base = jnp.where(core == 0, lax.dynamic_index_in_dim(w_gate, own, 0, False), lax.dynamic_index_in_dim(w_down_t, own, 0, False))
    base_up = lax.dynamic_index_in_dim(w_up, own, 0, False)

    def over_line(total, name):
        bits = 2 * heads
        while bits < groups // 2:
            total = small(sum_kernel, shape(*total.shape), (total, exchange(total, bits)), 6 * total.size, name)
            bits *= 2
        return total, exchange(total, bits)

    first, first_other = over_line(first, "line_sum")
    second, second_other = over_line(second, "line_sum")
    first_other, query, base, base_up = lax.optimization_barrier((first_other, query, base, base_up))
    upper = small(up_sum_kernel, half_block, (first, first_other), 6 * size, "up_sum")
    args = (first, first_other, second, second_other, upper, exchange(upper, 1), base, base_up)
    kernel = functools.partial(newton_kernel, heads)
    fresh, first, second = small(kernel, [block, part_block, part_block], args, 30 * size, "newton")

    def apply(far, *args):
        return small(functools.partial(apply_kernel, far), shape(rows, head_dim), (query, *args), 20 * rows * head_dim, "apply")

    over_y, over_z = [exchange(x, 2) for x in (first, second)], [exchange(x, 4) for x in (first, second)]
    across = [exchange(over_y[0], 4), exchange(over_z[1], 2)]
    swapped = lambda blocks: (*blocks, *(exchange(x, 1) for x in blocks))
    piece = apply(0, fresh, exchange(fresh, 1))
    over_y, over_z, piece = lax.optimization_barrier((over_y, over_z, piece))
    args = (query, piece, *swapped(over_y), *swapped(over_z))
    shapes = [shape(rows, 2 * head_dim), shape(rows, head_dim)]
    pieces = small(apply_two_kernel, shapes, args, 40 * rows * head_dim, "apply_two")
    return finish(query, pieces, swapped(across))


def solution(mesh):
    placed = (P(("scene", "tok"), None), P(), P(), P(), P(), P("scene"))
    return jax.shard_map(
        shards, mesh=mesh, in_specs=placed, out_specs=P(("scene", "tok"), None), check_vma=False
    )
```

```python
import functools

import jax
import jax.numpy as jnp
from jax import lax
from jax.experimental import pallas as pl
from jax.experimental.pallas import tpu as pltpu
from jax.sharding import PartitionSpec as P

VIEWS = 16
NS_STEPS = 5
BF16 = jnp.bfloat16
F32 = jnp.float32
K1_LIMIT = 40
SMALL_LIMIT = 24
FINISH_LOTS = 2

coef_a = 3.4445
coef_b = -4.775
coef_c = 2.0315
step_size = 0.8


def mm(a, b, dims):
    return lax.dot_general(a, b, (dims, ((), ())), preferred_element_type=F32)


NN = ((1,), (0,))
NT = ((1,), (1,))
TN = ((0,), (0,))


def position(heads):
    place = lax.axis_index("tok")
    return lax.rem(lax.div(place, 2), heads), lax.rem(place, 2)


def grad_kernel(
    view_hbm, tok_hbm, qkv_hbm, gate_hbm, up_hbm, down_hbm, first_keep_ref, second_keep_ref, first_give_ref, second_give_ref, view, tok, wkv, fast, kv, both_w, down_w, sems
):
    rows, width = tok.shape
    heads, head_dim = kv.shape[1], kv.shape[3]
    hidden = down_w.shape[2]
    half = head_dim // 2
    own, core = position(heads)
    owner = lax.div(lax.axis_index("tok") * rows, rows * lax.axis_size("tok") // VIEWS)
    count = iter(range(4 + 3 * heads))

    def fetch(source, target):
        copy = pltpu.make_async_copy(source, target, sems.at[next(count)])
        copy.start()
        return copy

    tok_copy = fetch(tok_hbm, tok)
    kv_copies = [fetch(qkv_hbm.at[:, (1 + which) * width : (2 + which) * width], wkv.at[which]) for which in range(2)]
    view_copy = fetch(view_hbm, view)
    fast_copies = [
        fetch(ref.at[head], fast.at[head, i]) for head in range(heads) for i, ref in enumerate((gate_hbm, up_hbm, down_hbm))
    ]
    tok_copy.wait()
    view_copy.wait()
    flag = view[owner].astype(F32)
    for which in range(2):
        kv_copies[which].wait()
        for pair in range(heads // 2):
            columns = slice(2 * pair * head_dim, (2 * pair + 2) * head_dim)
            part = mm(tok[...], wkv[which, :, columns], NN)
            part = (part * flag if which == 1 else part).astype(BF16)
            kv[which, 2 * pair] = part[:, :head_dim]
            kv[which, 2 * pair + 1] = part[:, head_dim:]
    for copy in fast_copies:
        copy.wait()
    for head in range(heads):
        both_w[head, :, :hidden] = fast[head, 0].astype(BF16)
        both_w[head, :, hidden:] = fast[head, 1].astype(BF16)
        down_w[head] = (-fast[head, 2]).astype(BF16)
    even = core == 0
    chunk = rows
    for head in range(heads):
        both_sum = down_sum = None
        for start in range(0, rows, chunk):
            k = kv[0, head, start : start + chunk, :]
            v = kv[1, head, start : start + chunk, :]
            both = mm(k, both_w[head], NN)
            dhid = mm(v, down_w[head], NN)
            gate, upper = both[:, :hidden], both[:, hidden:]
            sig = jax.nn.sigmoid(gate)
            act = gate * sig
            hid = (act * upper).astype(BF16)
            dgate = (dhid * upper * (sig + act * (1.0 - sig))).astype(BF16)
            dup = (dhid * act).astype(BF16)
            both_part = mm(k, jnp.concatenate([dgate, dup], axis=1), TN)
            down_part = mm(v, hid, TN)
            both_sum = both_part if both_sum is None else both_sum + both_part
            down_sum = down_part if down_sum is None else down_sum + down_part
        gate_g = both_sum[:, :hidden].astype(BF16)
        up_g = both_sum[:, hidden:].astype(BF16)
        down_g = (-down_sum).astype(BF16)
        slot = own ^ head
        keep = jnp.concatenate([jnp.where(even, up_g[:half], up_g[half:]), jnp.where(even, gate_g, down_g)], axis=0)
        give = jnp.concatenate([jnp.where(even, up_g[half:], up_g[:half]), jnp.where(even, down_g, gate_g)], axis=0)
        cut = keep.shape[0] // 2
        first_keep_ref[slot], second_keep_ref[slot] = keep[:cut], keep[cut:]
        first_give_ref[slot], second_give_ref[slot] = give[:cut], give[cut:]


def gradients(view_kind, tokens, qkv_weight, w_gate, w_up, w_down_t):
    rows, width = tokens.shape
    heads, head_dim, hidden = w_gate.shape
    args = [pltpu.with_memory_space_constraint(x, pltpu.HBM) for x in (view_kind, tokens, qkv_weight, w_gate, w_up, w_down_t)]
    shape = pltpu.VMEM((heads, head_dim * 3 // 4, hidden), BF16)
    return pl.pallas_call(
        grad_kernel,
        out_shape=[shape] * 4,
        in_specs=[pl.BlockSpec(memory_space=pl.ANY)] * 6,
        out_specs=[pl.BlockSpec(memory_space=pltpu.VMEM)] * 4,
        scratch_shapes=[
            pltpu.SMEM(view_kind.shape, jnp.int32),
            pltpu.VMEM((rows, width), BF16),
            pltpu.VMEM((2, width, width), BF16),
            pltpu.VMEM((heads, 3, head_dim, hidden), F32),
            pltpu.VMEM((2, heads, rows, head_dim), BF16),
            pltpu.VMEM((heads, head_dim, 2 * hidden), BF16),
            pltpu.VMEM((heads, head_dim, hidden), BF16),
            pltpu.SemaphoreType.DMA((4 + 3 * heads,)),
        ],
        compiler_params=pltpu.CompilerParams(vmem_limit_bytes=K1_LIMIT * 1024 * 1024),
        cost_estimate=pl.CostEstimate(
            flops=4 * rows * width * width + 12 * heads * rows * head_dim * hidden,
            bytes_accessed=2 * rows * width + 4 * width * width + 12 * heads * head_dim * hidden,
            transcendentals=heads * rows * hidden,
        ),
        name="gradients",
    )(*args)


def small(kernel, shapes, operands, nbytes, name):
    specs = [pl.BlockSpec(memory_space=pltpu.VMEM)] * len(operands)
    operands = [pltpu.with_memory_space_constraint(x, pltpu.VMEM) for x in operands]
    return pl.pallas_call(
        kernel,
        out_shape=shapes,
        in_specs=specs,
        compiler_params=pltpu.CompilerParams(vmem_limit_bytes=SMALL_LIMIT * 1024 * 1024),
        cost_estimate=pl.CostEstimate(flops=0, bytes_accessed=nbytes, transcendentals=0),
        name=name,
    )(*operands)


def query_kernel(tokens_ref, weight_ref, out_ref):
    heads, _, head_dim = out_ref.shape
    part = mm(tokens_ref[...], weight_ref[...], NN).astype(BF16)
    for head in range(heads):
        out_ref[head] = part[:, head * head_dim : (head + 1) * head_dim]


def project_query(tokens, weight, heads):
    rows, width = tokens.shape
    return pl.pallas_call(
        query_kernel,
        out_shape=pltpu.VMEM((heads, rows, width // heads), BF16),
        grid=(1,),
        in_specs=[pl.BlockSpec((rows, width), lambda i: (0, 0)), pl.BlockSpec((width, width), lambda i: (0, 0))],
        out_specs=pl.BlockSpec((heads, rows, width // heads), lambda i: (0, 0, 0)),
        compiler_params=pltpu.CompilerParams(vmem_limit_bytes=SMALL_LIMIT * 1024 * 1024),
        cost_estimate=pl.CostEstimate(flops=2 * rows * width * width, bytes_accessed=4 * width * (rows + width), transcendentals=0),
        name="query",
    )(*(pltpu.with_memory_space_constraint(x, pltpu.HBM) for x in (tokens, weight)))


def pair_sum_kernel(keep_ref, got_ref, *out_refs):
    for slot, out_ref in enumerate(out_refs):
        out_ref[...] = (keep_ref[slot].astype(F32) + got_ref[slot].astype(F32)).astype(BF16)


def up_sum_kernel(mine_ref, other_ref, out_ref):
    half = out_ref.shape[0]
    out_ref[...] = (mine_ref[:half].astype(F32) + other_ref[:half].astype(F32)).astype(BF16)


def sum_kernel(*refs):
    *parts, out_ref = refs
    total = parts[0][...].astype(F32)
    for part in parts[1:]:
        total = total + part[...].astype(F32)
    out_ref[...] = total.astype(BF16)


def stepped(totals, bases):
    norms = [jnp.sqrt(jnp.sum(total * total)) for total in totals]
    iterates = [(total / (norm + 1e-07)).astype(BF16) for total, norm in zip(totals, norms)]
    for step in range(NS_STEPS):
        grams = [mm(x, x, NT).astype(BF16) for x in iterates]
        squares = [mm(g, g, NN) for g in grams]
        mixers = [(coef_b * g.astype(F32) + coef_c * s).astype(BF16) for g, s in zip(grams, squares)]
        moved = [mm(m, x, NN) for m, x in zip(mixers, iterates)]
        iterates = [(coef_a * x.astype(F32) + y).astype(BF16) for x, y in zip(iterates, moved)]
    return [(base - step_size * x.astype(F32)).astype(BF16) for base, x in zip(bases, iterates)]


def newton_kernel(
    heads, first_ref, first_other_ref, second_ref, second_other_ref, half_ref, got_ref, base_ref, base_up_ref, out_ref, *part_refs
):
    half = half_ref.shape[0]
    even = position(heads)[1] == 0
    a, b = half_ref[...], got_ref[...]
    upper = jnp.concatenate([jnp.where(even, a, b), jnp.where(even, b, a)], axis=0).astype(F32)
    first = first_ref[half:].astype(F32) + first_other_ref[half:].astype(F32)
    second = second_ref[...].astype(F32) + second_other_ref[...].astype(F32)
    main, upper = stepped((jnp.concatenate([first, second], axis=0), upper), (base_ref[...], base_up_ref[...]))
    whole = jnp.concatenate([jnp.where(even, upper[:half], upper[half:]), main], axis=0)
    out_ref[...] = whole
    rows = whole.shape[0] // len(part_refs)
    for index, part_ref in enumerate(part_refs):
        part_ref[...] = whole[index * rows : (index + 1) * rows]


def head_output(even, q, here, there):
    head_dim = q.shape[1]
    here, there = (jnp.concatenate([ref[...] for ref in refs], axis=0) for refs in (here, there))
    a, b = jnp.where(even, here, there), jnp.where(even, there, here)
    half = head_dim // 2
    up_b = jnp.concatenate([a[:half], b[:half]], axis=0)
    gate = mm(q, a[half:], NN)
    upper = mm(q, up_b, NN)
    hidden = (gate * jax.nn.sigmoid(gate) * upper).astype(BF16)
    return mm(hidden, b[half:], NT).astype(BF16)


def apply_kernel(far, q_ref, *refs):
    *block_refs, out_ref = refs
    half = len(block_refs) // 2
    own, core = position(q_ref.shape[0])
    out_ref[...] = head_output(core == 0, q_ref[own ^ far], block_refs[:half], block_refs[half:])


def beside(even_head, a, b):
    return jnp.concatenate([jnp.where(even_head, a, b), jnp.where(even_head, b, a)], axis=1)


def apply_two_kernel(q_ref, piece_ref, *refs):
    *block_refs, pair_ref, far_ref = refs
    count = len(block_refs) // 4
    own, core = position(q_ref.shape[0])
    lots = [block_refs[i * count : (i + 1) * count] for i in range(4)]
    near = head_output(core == 0, q_ref[own ^ 1], lots[0], lots[1])
    pair_ref[...] = beside(lax.rem(own, 2) == 0, piece_ref[...], near)
    far_ref[...] = head_output(core == 0, q_ref[own ^ 2], lots[2], lots[3])


def finish_kernel(q_ref, pair_ref, far_ref, first_ref, second_ref, first_there_ref, second_there_ref, out_hbm, other, sems):
    heads, rows, head_dim = q_ref.shape
    own, core = position(heads)
    pair = lax.div(own, 2)
    lot = rows // FINISH_LOTS
    columns = [pl.ds(pl.multiple_of(p * 2 * head_dim, 128), 2 * head_dim) for p in (pair, pair ^ 1)]
    copies = [pltpu.make_async_copy(pair_ref, out_hbm.at[:, columns[0]], sems.at[FINISH_LOTS])]
    copies[0].start()
    for index in range(FINISH_LOTS):
        part = pl.ds(index * lot, lot)
        q = q_ref[own ^ (heads - 1), part]
        last = head_output(core == 0, q, (first_ref, second_ref), (first_there_ref, second_there_ref))
        other[part] = beside(lax.rem(own, 2) == 0, far_ref[part], last)
        copies.append(pltpu.make_async_copy(other.at[part], out_hbm.at[part, columns[1]], sems.at[index]))
        copies[-1].start()
    for copy in copies:
        copy.wait()


def finish(query, pieces, blocks):
    heads, rows, head_dim = query.shape
    operands = [pltpu.with_memory_space_constraint(x, pltpu.VMEM) for x in (query, *pieces, *blocks)]
    return pl.pallas_call(
        finish_kernel,
        out_shape=jax.ShapeDtypeStruct((rows, heads * head_dim), BF16),
        in_specs=[pl.BlockSpec(memory_space=pltpu.VMEM)] * len(operands),
        out_specs=pl.BlockSpec(memory_space=pl.ANY),
        scratch_shapes=[
            pltpu.VMEM((rows, 2 * head_dim), BF16),
            pltpu.SemaphoreType.DMA((FINISH_LOTS + 1,)),
        ],
        compiler_params=pltpu.CompilerParams(vmem_limit_bytes=SMALL_LIMIT * 1024 * 1024),
        name="finish",
    )(*operands)


def shards(tokens, qkv_weight, w_gate, w_up, w_down, view_kind):
    rows, width = tokens.shape
    heads, head_dim, hidden = w_gate.shape
    groups = lax.axis_size("tok")
    own, core = position(heads)
    w_down_t = jnp.transpose(w_down, (0, 2, 1))
    half = head_dim // 2
    shape = lambda *dims: pltpu.VMEM(dims, BF16)
    size = head_dim * hidden
    main_block, half_block = shape(head_dim, hidden), shape(half, hidden)
    size = head_dim * hidden

    def exchange(x, bits):
        return lax.ppermute(x, "tok", [(i, i ^ bits) for i in range(groups)])

    first, second, first_give, second_give = gradients(view_kind, tokens, qkv_weight, w_gate, w_up, w_down_t)
    block, part_block = shape(head_dim + half, hidden), shape((head_dim + half) // 2, hidden)
    first, second = (
        small(pair_sum_kernel, [part_block] * heads, (keep, exchange(give, 1)), 9 * keep.size, "pair_sum")
        for keep, give in ((first, first_give), (second, second_give))
    )
    first_on, second_on = exchange(first[3], 4), exchange(second[3], 2)
    first_in, second_in = exchange(first[2], 4), exchange(second[1], 2)
    first_on = exchange(small(sum_kernel, part_block, (first[1], first_on), 6 * size, "pass_sum"), 2)
    second_on = exchange(small(sum_kernel, part_block, (second[2], second_on), 6 * size, "pass_sum"), 4)
    first = small(sum_kernel, part_block, (first[0], first_in, first_on), 8 * size, "plane_sum")
    second = small(sum_kernel, part_block, (second[0], second_in, second_on), 8 * size, "plane_sum")
    query = project_query(tokens, qkv_weight, heads)
    base = jnp.where(core == 0, lax.dynamic_index_in_dim(w_gate, own, 0, False), lax.dynamic_index_in_dim(w_down_t, own, 0, False))
    base_up = lax.dynamic_index_in_dim(w_up, own, 0, False)

    def over_line(total, name):
        bits = 2 * heads
        while bits < groups // 2:
            total = small(sum_kernel, shape(*total.shape), (total, exchange(total, bits)), 6 * total.size, name)
            bits *= 2
        return total, exchange(total, bits)

    first, first_other = over_line(first, "line_sum")
    second, second_other = over_line(second, "line_sum")
    first_other, query, base, base_up = lax.optimization_barrier((first_other, query, base, base_up))
    upper = small(up_sum_kernel, half_block, (first, first_other), 6 * size, "up_sum")
    args = (first, first_other, second, second_other, upper, exchange(upper, 1), base, base_up)
    kernel = functools.partial(newton_kernel, heads)
    fresh, first, second = small(kernel, [block, part_block, part_block], args, 30 * size, "newton")

    def apply(far, *args):
        return small(functools.partial(apply_kernel, far), shape(rows, head_dim), (query, *args), 20 * rows * head_dim, "apply")

    over_y, over_z = [exchange(x, 2) for x in (first, second)], [exchange(x, 4) for x in (first, second)]
    across = [exchange(over_z[0], 2), exchange(over_y[1], 4)]
    swapped = lambda blocks: (*blocks, *(exchange(x, 1) for x in blocks))
    piece = apply(0, fresh, exchange(fresh, 1))
    over_y, over_z, piece = lax.optimization_barrier((over_y, over_z, piece))
    args = (query, piece, *swapped(over_y), *swapped(over_z))
    shapes = [shape(rows, 2 * head_dim), shape(rows, head_dim)]
    pieces = small(apply_two_kernel, shapes, args, 40 * rows * head_dim, "apply_two")
    return finish(query, pieces, swapped(across))


def solution(mesh):
    placed = (P(("scene", "tok"), None), P(), P(), P(), P(), P("scene"))
    return jax.shard_map(
        shards, mesh=mesh, in_specs=placed, out_specs=P(("scene", "tok"), None), check_vma=False
    )
```
